512 devices in a mesh: grp: 4 (over z_hi, core), seq: 32 (over y, z_lo), tp: 4 (over x).
Axes of the slice: x: 4, y: 4, z: 16 (z_hi: 2, z_lo: 8; z = z_hi * 8 + z_lo), core: 2. Of those that a mesh axis runs over, the one named last changes fastest.
Arguments:
- student_hidden_states: bfloat16 [4096, 5120], P('seq'), may hold values from -6 to 6
- student_norm_gain: float32 [5120], replicated, may hold values from 0.25 to 1.75
- student_output_head: bfloat16 [5120, 64], replicated, may hold values from -0.078125 to 0.078125
- noise: bfloat16 [4096, 64], P('seq'), may hold values from -6 to 6
- timestep: int32 [1], replicated, may hold values from 20 to 979
- context: bfloat16 [4096, 5120], P('seq'), may hold values from -80 to 80
- patch_embedding_input: bfloat16 [64, 5120], replicated, may hold values from -0.75 to 0.75
- attention_norm_gain: float32 [5120], replicated, may hold values from 0.25 to 1.75
- query_weight: bfloat16 [5120, 4096], P('seq', ('grp', 'tp')), may hold values from -1 to 1
- key_weight: bfloat16 [5120, 4096], P('seq', ('grp', 'tp')), may hold values from -1 to 1
- value_weight: bfloat16 [5120, 4096], P('seq', ('grp', 'tp')), may hold values from -0.078125 to 0.078125
- adapter_down_weight: bfloat16 [5120, 64], P('seq'), may hold values from -0.078125 to 0.078125
- adapter_up_weight: bfloat16 [64, 4096], P(None, ('grp', 'tp')), may hold values from -0.75 to 0.75
- output_weight: bfloat16 [4096, 5120], P(('grp', 'tp'), 'seq'), may hold values from -0.09375 to 0.09375
- velocity_head_output: bfloat16 [5120, 64], replicated, may hold values from -0.078125 to 0.078125
Outputs:
- dmd_grad: float32 [4096, 64], P('seq')
- head_grad: float32 [5120, 64], P(('grp', 'tp'))
The draws below stay inside these ranges and needn't reach their ends.
All inputs are finite; a program needn't handle non-finite values. Where the reference program divides by a largest or mean magnitude, that divisor is 1e-20 or more.
Results may differ from the reference program's by a relative error of at most 0.015.
The reference program's roundings to bfloat16 on the way count: a program that leaves them out, or rounds other values in their place, can miss the bound.
Values may be sent and summed in bfloat16 or wider, within the bound.
A program may use at most 64 MiB of HBM per device.

```python
import jax
import jax.numpy as jnp
from jax import lax

MODEL_WIDTH = 5120
ATTENTION_HEADS = 32
HEAD_WIDTH = 128
LAT = 64
ADAPTER_RANK = 64
SEQ = 4096


def draw_query_weight(key, part):
    key = jax.random.fold_in(key, 1)
    base = jnp.clip(jax.random.normal(key, (MODEL_WIDTH, ATTENTION_HEADS * HEAD_WIDTH), jnp.float32), -6.0, 6.0) * MODEL_WIDTH ** (-0.5)
    return base.astype(jnp.bfloat16)


def draw_key_weight(key, part):
    key = jax.random.fold_in(key, 2)
    base = jnp.clip(jax.random.normal(key, (MODEL_WIDTH, ATTENTION_HEADS * HEAD_WIDTH), jnp.float32), -6.0, 6.0) * MODEL_WIDTH ** (-0.5)
    return base.astype(jnp.bfloat16)


def draw_context(key, part):
    key = jax.random.fold_in(key, 3)
    base = jnp.clip(jax.random.normal(key, (SEQ, MODEL_WIDTH), jnp.float32), -6.0, 6.0)
    return base.astype(jnp.bfloat16)


def block_scale(stream_key, extent, cuts, low, largest):
    factor_of = 1.0
    for dim, parts in cuts:
        draws = jax.random.uniform(jax.random.fold_in(jax.random.fold_in(stream_key, 6), dim), (parts,), jnp.float32, low / len(cuts), largest / len(cuts))
        factor_of = factor_of * jnp.repeat(jnp.exp(draws), extent[dim] // parts).reshape((-1,) + (1,) * (len(extent) - 1 - dim))
    return factor_of


def gaussian(rng, extent, deviation, limit, cuts=(), held_as=jnp.bfloat16):
    factor_of = block_scale(rng, extent, cuts, -0.22, 0.18) if cuts else 1.0
    result = jax.random.normal(rng, extent, jnp.float32) * deviation * factor_of
    return jnp.minimum(jnp.maximum(result, -limit), limit).astype(held_as)


def setup_inputs(seed: int = 0) -> dict:
    seeds = jax.random.split(jax.random.key(seed), 16)
    return {
        "student_hidden_states": gaussian(seeds[0], (SEQ, MODEL_WIDTH), 1.0, 6.0, ((0, 32),)),
        "student_norm_gain": jnp.clip(1.0 + 0.15 * jax.random.normal(seeds[1], (MODEL_WIDTH,), jnp.float32), 0.25, 1.75),
        "student_output_head": gaussian(seeds[2], (MODEL_WIDTH, LAT), MODEL_WIDTH ** -0.5, 0.078125),
        "noise": gaussian(seeds[3], (SEQ, LAT), 1.0, 6.0, ((0, 32),)),
        "timestep": jax.random.randint(seeds[4], (1,), 20, 980).astype(jnp.int32),
        "context": draw_context(jax.random.fold_in(seeds[15], 71), 0),
        "patch_embedding_input": gaussian(seeds[6], (LAT, MODEL_WIDTH), LAT ** -0.5, 0.75),
        "attention_norm_gain": jnp.clip(1.0 + 0.15 * jax.random.normal(seeds[7], (MODEL_WIDTH,), jnp.float32), 0.25, 1.75),
        "query_weight": draw_query_weight(jax.random.fold_in(seeds[15], 71), 0),
        "key_weight": draw_key_weight(jax.random.fold_in(seeds[15], 71), 0),
        "value_weight": gaussian(seeds[10], (MODEL_WIDTH, ATTENTION_HEADS * HEAD_WIDTH), MODEL_WIDTH ** -0.5, 0.078125, ((0, 32), (1, 16))),
        "adapter_down_weight": gaussian(seeds[11], (MODEL_WIDTH, ADAPTER_RANK), MODEL_WIDTH ** -0.5, 0.078125, ((0, 32),)),
        "adapter_up_weight": gaussian(seeds[12], (ADAPTER_RANK, ATTENTION_HEADS * HEAD_WIDTH), ADAPTER_RANK ** -0.5, 0.75, ((1, 16),)),
        "output_weight": gaussian(seeds[13], (ATTENTION_HEADS * HEAD_WIDTH, MODEL_WIDTH), (ATTENTION_HEADS * HEAD_WIDTH) ** -0.5, 0.09375, ((0, 16), (1, 32))),
        "velocity_head_output": gaussian(seeds[14], (MODEL_WIDTH, LAT), MODEL_WIDTH ** -0.5, 0.078125),
    }


def rms_norm(values):
    return values * lax.rsqrt(lax.optimization_barrier(jnp.mean(values * values, axis=-1, keepdims=True)) + 1e-06)

def attend_head(operands):
    query_teacher, query_fake, key_head, value_head = operands
    outputs = []
    for query_head in (query_teacher, query_fake):
        scores = jnp.dot(query_head, key_head.T, preferred_element_type=jnp.float32) * HEAD_WIDTH ** (-0.5)
        top_score = lax.optimization_barrier(jnp.max(scores, axis=-1, keepdims=True))
        expo = jnp.exp(scores - top_score)
        total = lax.optimization_barrier(jnp.sum(expo, axis=-1, keepdims=True))
        mixed = jnp.dot(expo.astype(jnp.bfloat16), value_head, preferred_element_type=jnp.float32)
        outputs.append((mixed / total).astype(jnp.bfloat16))
    return (outputs[0], outputs[1])

def split_heads(matrix):
    return matrix.reshape(matrix.shape[0], ATTENTION_HEADS, HEAD_WIDTH).transpose(1, 0, 2)

def join_heads(tensor):
    return tensor.transpose(1, 0, 2).reshape(tensor.shape[1], ATTENTION_HEADS * HEAD_WIDTH)

def reference(student_hidden_states, student_norm_gain, student_output_head, noise, timestep, context, patch_embedding_input, attention_norm_gain, query_weight, key_weight, value_weight, adapter_down_weight, adapter_up_weight, output_weight, velocity_head_output):
    fraction = timestep[0].astype(jnp.float32) / 1000.0
    noise_level = 5.0 * fraction / (1.0 + 4.0 * fraction)
    act_student = (rms_norm(student_hidden_states.astype(jnp.float32)) * student_norm_gain).astype(jnp.bfloat16)
    latent = jnp.dot(act_student, student_output_head, preferred_element_type=jnp.float32)
    noisy = ((1.0 - noise_level) * latent + noise_level * noise.astype(jnp.float32)).astype(jnp.bfloat16)
    hidden = jnp.dot(noisy, patch_embedding_input, preferred_element_type=jnp.float32) + context.astype(jnp.float32)
    activation = (rms_norm(hidden) * attention_norm_gain).astype(jnp.bfloat16)
    adapter_lowrank = jnp.dot(activation, adapter_down_weight, preferred_element_type=jnp.float32).astype(jnp.bfloat16)
    complete_query = jnp.dot(activation, query_weight, preferred_element_type=jnp.float32)
    q_teacher = complete_query.astype(jnp.bfloat16)
    fake_query_rows = (complete_query + jnp.dot(adapter_lowrank, adapter_up_weight, preferred_element_type=jnp.float32)).astype(jnp.bfloat16)
    keys = jnp.dot(activation, key_weight, preferred_element_type=jnp.float32).astype(jnp.bfloat16)
    values = jnp.dot(activation, value_weight, preferred_element_type=jnp.float32).astype(jnp.bfloat16)
    att_teacher, att_fake = lax.map(attend_head, (split_heads(q_teacher), split_heads(fake_query_rows), split_heads(keys), split_heads(values)))
    head_float = velocity_head_output.astype(jnp.float32)
    velocity = []
    for attended in (att_teacher, att_fake):
        branch = jnp.dot(join_heads(attended), output_weight, preferred_element_type=jnp.float32)
        velocity.append(jnp.dot(hidden + branch, head_float, precision=lax.Precision.HIGHEST))
    noisy_float = noisy.astype(jnp.float32)
    real_pred = noisy_float - noise_level * velocity[0]
    fake_pred = noisy_float - noise_level * velocity[1]
    diff = fake_pred - real_pred
    norm_scale = 1.0 / (jnp.mean(jnp.abs(latent - real_pred)) + 1e-05)
    dmd_grad = norm_scale * diff
    token_scale = 1.0 / jnp.sqrt(jnp.float32(SEQ))
    head_grad = norm_scale * token_scale * jnp.dot(act_student.astype(jnp.float32).T, diff, precision=lax.Precision.HIGHEST)
    return (dmd_grad, head_grad)
```

```python
import functools

import jax
import jax.numpy as jnp
from jax import lax
from jax.experimental import pallas as pl
from jax.experimental.pallas import tpu as pltpu
from jax.sharding import PartitionSpec as P

HEAD_WIDTH = 128
LAT = 64
COLUMNS = 4
EPS = 1e-06
F32 = jnp.float32
BF16 = jnp.bfloat16
MIB = 1024 * 1024


def position(rows_z):
    seq = lax.axis_index("seq")
    y, z = seq // rows_z, seq % rows_z
    side = y // 2
    pair = jnp.where(y < 2, y, 3 - y)
    partner = (3 - y) * rows_z + z
    sibling = (y + 1 - 2 * (y % 2)) * rows_z + z
    return seq, y, z, side, pair, partner, sibling


def copy_to(src, dst, send_sem, recv_sem, target):
    return pltpu.make_async_remote_copy(
        src_ref=src,
        dst_ref=dst,
        send_sem=send_sem,
        recv_sem=recv_sem,
        device_id=target,
        device_id_type=pl.DeviceIdType.MESH,
    )


class Chain:
    def __init__(self, unit, send_sem, recv_sem, rows_z):
        self.unit, self.send_sem, self.recv_sem, self.rows_z = unit, send_sem, recv_sem, rows_z
        (self.seq, _, self.z, _, self.pair, _, self.sibling) = position(rows_z)

    def copy(self, pair, row, way, target):
        ref = self.unit(pair, row)
        return copy_to(
            ref,
            ref,
            self.send_sem.at[way * self.rows_z + row],
            self.recv_sem.at[pair * self.rows_z + row],
            {"seq": target},
        )

    def up(self, row):
        return self.copy(self.pair, row, 0, jnp.minimum(self.seq + 1, 4 * self.rows_z - 1))

    def down(self, row):
        return self.copy(self.pair, row, 1, jnp.maximum(self.seq - 1, 0))

    def across(self, row):
        return self.copy(self.pair, row, 2, self.sibling)

    def own(self):
        z = self.z

        @pl.when(z < self.rows_z - 1)
        def _():
            self.up(z).start()

        @pl.when(z > 0)
        def _():
            self.down(z).start()

        self.across(z).start()

    def step(self, t):
        z, last = self.z, self.rows_z - 1

        @pl.when(z - t >= 0)
        def _():
            row = z - t
            self.up(row).wait_recv()

            @pl.when(z < last)
            def _():
                self.up(row).start()

            self.across(row).start()

        @pl.when(z + t <= last)
        def _():
            row = z + t
            self.down(row).wait_recv()

            @pl.when(z > 0)
            def _():
                self.down(row).start()

            self.across(row).start()

    def forward(self):
        def body(t, carry):
            self.step(t)
            return carry

        lax.fori_loop(1, self.rows_z, body, 0)

    def sibling_recv(self):
        def body(row, carry):
            self.copy(1 - self.pair, row, 2, self.sibling).wait_recv()
            return carry

        lax.fori_loop(0, self.rows_z, body, 0)

    def drain(self):
        z, last = self.z, self.rows_z - 1

        def body(row, carry):
            @pl.when(jnp.logical_and(z < last, row <= z))
            def _():
                self.up(row).wait_send()

            @pl.when(jnp.logical_and(z > 0, row >= z))
            def _():
                self.down(row).wait_send()

            self.across(row).wait_send()
            return carry

        lax.fori_loop(0, self.rows_z, body, 0)


def noise_level_of(timestep_ref):
    fraction = jnp.full((1, LAT), timestep_ref[0], jnp.int32).astype(F32) / 1000.0
    return 5.0 * fraction / (1.0 + 4.0 * fraction)


def three_parts(value):
    high = value.astype(BF16)
    rest = value - high.astype(F32)
    middle = rest.astype(BF16)
    low = (rest - middle.astype(F32)).astype(BF16)
    return high, middle, low


def main_kernel(
    rows_z,
    timestep_ref,
    student_ref,
    student_gain_ref,
    student_head_ref,
    noise_ref,
    context_ref,
    patch_ref,
    gain_ref,
    query_ref,
    key_ref,
    value_ref,
    down_ref,
    up_ref,
    output_ref,
    velocity_ref,
    share_ref,
    aux_ref,
    block_ref,
    weights,
    staged,
    act_student,
    hidden,
    act,
    queries,
    kv,
    scores,
    top,
    total,
    mixed,
    w_send,
    w_recv,
    kv_send,
    kv_recv,
    swap_send,
    swap_recv,
    act_send,
    act_recv,
):
    seq, y, z, side, pair, partner, sibling = position(rows_z)
    tokens, width = student_ref.shape
    depth = query_ref.shape[0]
    groups = lax.axis_size("grp") * lax.axis_size("tp")
    group = lax.axis_index("grp") * lax.axis_size("tp") + lax.axis_index("tp")

    barrier = pltpu.get_barrier_semaphore()

    def greet(target):
        pl.semaphore_signal(
            barrier, inc=1, device_id={"seq": target}, device_id_type=pl.DeviceIdType.MESH
        )

    greet(partner)
    greet(sibling)

    @pl.when(z > 0)
    def _():
        greet(jnp.maximum(seq - 1, 0))

    @pl.when(z < rows_z - 1)
    def _():
        greet(jnp.minimum(seq + 1, 4 * rows_z - 1))

    velocity_rows = velocity_ref[pl.ds(pl.multiple_of(seq * depth, 16), depth), :]
    for which in range(2):
        head = side if which == 0 else 1 - side
        columns = pl.ds(pl.multiple_of(head * HEAD_WIDTH, HEAD_WIDTH), HEAD_WIDTH)
        folded = jnp.dot(
            output_ref[columns, :], velocity_rows, preferred_element_type=F32
        ).astype(BF16)
        rows = folded.shape[0]
        if depth > rows:
            folded = jnp.concatenate([folded, jnp.zeros((depth - rows, LAT), BF16)], axis=0)
        last = jnp.concatenate([down_ref[...], folded], axis=1)
        slot = weights.at[2 * pair + side, z] if which == 0 else staged
        slot[:, 0:128] = query_ref[:, columns]
        slot[:, 128:256] = key_ref[:, columns]
        slot[:, 256:384] = value_ref[:, columns]
        slot[:, 384:512] = last

    @pl.when(jnp.logical_and(z > 0, z < rows_z - 1))
    def _():
        pl.semaphore_wait(barrier, 4)

    @pl.when(jnp.logical_or(z == 0, z == rows_z - 1))
    def _():
        pl.semaphore_wait(barrier, 3)

    swap = copy_to(
        staged, weights.at[2 * pair + side, z], swap_send, swap_recv, {"seq": partner}
    )
    swap.start()

    chunk = 16

    def student_rows(i, carry):
        rows = pl.ds(pl.multiple_of(i * chunk, chunk), chunk)
        value = student_ref[rows, :].astype(F32)
        scale = lax.rsqrt(jnp.mean(value * value, axis=-1, keepdims=True) + EPS)
        act_student[rows, :] = (value * scale * student_gain_ref[...]).astype(BF16)
        return carry

    lax.fori_loop(0, tokens // chunk, student_rows, 0)

    copy_to(
        staged, weights.at[2 * pair + 1 - side, z], swap_send, swap_recv, {"seq": partner}
    ).wait_recv()
    w_chain = Chain(lambda p, r: weights.at[pl.ds(2 * p, 2), r], w_send, w_recv, rows_z)
    w_chain.own()

    level = noise_level_of(timestep_ref)
    latent = jnp.dot(act_student[...], student_head_ref[...], preferred_element_type=F32)
    noisy = ((1.0 - level) * latent + level * noise_ref[...].astype(F32)).astype(BF16)
    slab = 512 if width % 512 == 0 else width

    def hidden_columns(i, carry):
        columns = pl.ds(pl.multiple_of(i * slab, slab), slab)
        hidden[:, columns] = jnp.dot(
            noisy, patch_ref[:, columns], preferred_element_type=F32
        ) + context_ref[:, columns].astype(F32)
        return carry

    lax.fori_loop(0, width // slab, hidden_columns, 0)

    def act_rows(i, carry):
        value = hidden[pl.ds(pl.multiple_of(i * chunk, chunk), chunk), :]
        scale = lax.rsqrt(jnp.mean(value * value, axis=-1, keepdims=True) + EPS)
        act[side, pl.ds(pl.multiple_of(i * chunk, chunk), chunk), :] = (
            value * scale * gain_ref[...]
        ).astype(BF16)
        return carry

    lax.fori_loop(0, tokens // chunk, act_rows, 0)
    act_copy = copy_to(act.at[side], act.at[side], act_send, act_recv, {"seq": partner})
    act_copy.start()

    mine = pl.ds(pl.multiple_of(group * 8, 8), 8)
    queries[0, 0:tokens, 0:LAT] = latent
    queries[1, 0:tokens, 0:LAT] = noisy.astype(F32)
    parts = three_parts(hidden[mine, :])
    residual = sum(
        jnp.dot(part, velocity_ref[...], preferred_element_type=F32) for part in parts
    )
    aux_ref[0:8, :] = residual
    aux_ref[8:16, :] = queries[0, mine, 0:LAT]
    aux_ref[16:24, :] = queries[1, mine, 0:LAT]
    grad_rows = width // groups
    start = group * grad_rows
    if grad_rows % 128:
        start = start - (group % 2) * LAT
    block_ref[...] = act_student[
        :, pl.ds(pl.multiple_of(start, 128), block_ref.shape[1])
    ]

    w_chain.forward()
    w_chain.sibling_recv()
    copy_to(
        act.at[1 - side], act.at[1 - side], act_send, act_recv, {"seq": partner}
    ).wait_recv()

    both = jnp.concatenate([act[0], act[1]], axis=0)
    span = width // COLUMNS
    product = None
    for place, column in enumerate((0, 3, 1, 2)):
        term = jnp.dot(
            both[:, column * span : (column + 1) * span],
            weights[place].reshape(span, 512),
            preferred_element_type=F32,
        )
        product = term if product is None else product + term

    def fold_rows(r, carry):
        for place in range(COLUMNS):
            carry = carry + weights[place, r, 0 : min(depth, HEAD_WIDTH), 384:512].astype(F32)
        return carry

    folded = lax.fori_loop(
        0, rows_z, fold_rows, jnp.zeros((min(depth, HEAD_WIDTH), 128), F32)
    )[:, LAT:]
    high = folded.astype(BF16)
    low_part = (folded - high.astype(F32)).astype(BF16)
    values = product[:, 256:384].astype(BF16)
    moved = jnp.dot(
        values, jnp.concatenate([high, low_part], axis=1), preferred_element_type=F32
    )
    moved = (moved[:, :LAT] + moved[:, LAT:]).astype(BF16)
    kv[pair, z, 0 : 2 * tokens, :] = product[:, 128:256].astype(BF16)
    kv[pair, z, 2 * tokens : 3 * tokens, :] = jnp.concatenate(
        [moved[:tokens], moved[tokens:]], axis=1
    )
    kv_chain = Chain(lambda p, r: kv.at[p, r], kv_send, kv_recv, rows_z)
    kv_chain.own()

    low = product[:, 384 : 384 + LAT].astype(BF16)
    head_columns = pl.ds(pl.multiple_of(side * HEAD_WIDTH, HEAD_WIDTH), HEAD_WIDTH)
    plain = product[:, 0:128]
    queries[0] = plain
    queries[1] = plain + jnp.dot(low, up_ref[:, head_columns], preferred_element_type=F32)
    asked = jnp.concatenate([queries[0], queries[1]], axis=0).astype(BF16)

    kv_chain.forward()
    kv_chain.sibling_recv()

    top[...] = jnp.full(top.shape, -1e30, F32)
    factor = HEAD_WIDTH**-0.5

    def score_unit(u, carry):
        keys = kv[u // rows_z, u % rows_z, 0 : 2 * tokens, :]
        found = (
            lax.dot_general(asked, keys, (((1,), (1,)), ((), ())), preferred_element_type=F32)
            * factor
        )
        scores[u] = found
        top[...] = jnp.maximum(
            top[...], jnp.maximum(found[:, :tokens], found[:, tokens:])
        )
        return carry

    lax.fori_loop(0, 2 * rows_z, score_unit, 0)
    peak = jnp.max(top[...], axis=-1, keepdims=True)
    top[...] = jnp.broadcast_to(peak, top.shape)
    total[...] = jnp.zeros(total.shape, F32)
    mixed[...] = jnp.zeros(mixed.shape, F32)

    def mix_unit(u, carry):
        shift = top[...]
        left = jnp.exp(scores[u, :, 0:tokens] - shift)
        right = jnp.exp(scores[u, :, tokens : 2 * tokens] - shift)
        total[...] += left + right
        packed = kv[u // rows_z, u % rows_z, 2 * tokens : 3 * tokens, :]
        stacked = jnp.concatenate([packed[:, :LAT], packed[:, LAT:]], axis=0)
        mixed[...] += jnp.dot(
            jnp.concatenate([left, right], axis=1).astype(BF16),
            stacked,
            preferred_element_type=F32,
        )
        return carry

    lax.fori_loop(0, 2 * rows_z, mix_unit, 0)
    attended = mixed[...] / jnp.sum(total[...], axis=-1, keepdims=True)
    share_ref[...] = jnp.concatenate(
        [attended[: 2 * tokens], attended[2 * tokens :]], axis=1
    )

    swap.wait_send()
    act_copy.wait_send()
    w_chain.drain()
    kv_chain.drain()


def tail_kernel(
    rows_z,
    timestep_ref,
    share_ref,
    aux_ref,
    block_ref,
    diff_ref,
    grad_ref,
    met,
    tiles,
    window,
    outgoing,
    arrived,
    pieces,
    send1,
    recv1,
    send2,
    recv2,
    send3,
    recv3,
    send4,
    recv4,
):
    seq, y, z, side, pair, partner, sibling = position(rows_z)
    tp_size = lax.axis_size("tp")
    groups = lax.axis_size("grp") * tp_size
    group = lax.axis_index("grp") * tp_size + lax.axis_index("tp")
    seqs = 4 * rows_z
    tokens = 8 * groups
    grad_rows = grad_ref.shape[0]
    owners = grad_rows // 16
    me = side * groups + group

    def member(j):
        other = j // groups
        column = jnp.where(other == 0, pair, 3 - pair)
        g = j % groups
        return {"grp": g // tp_size, "seq": column * rows_z + z, "tp": g % tp_size}

    def peer(g):
        return {"grp": g // tp_size, "tp": g % tp_size}

    def each(count, skip, act):
        def body(j, carry):
            @pl.when(j != skip)
            def _():
                act(j)

            return carry

        lax.fori_loop(0, count, body, 0)

    barrier = pltpu.get_barrier_semaphore()

    def greet(target):
        pl.semaphore_signal(
            barrier, inc=1, device_id=target, device_id_type=pl.DeviceIdType.MESH
        )

    each(2 * groups, me, lambda j: greet(member(j)))

    def greet_seq(p):
        @pl.when(p != partner)
        def _():
            greet({"seq": p})

    each(seqs, seq, greet_seq)
    pl.semaphore_wait(barrier, 2 * groups - 1 + seqs - 2)

    def rows_of(j):
        return share_ref.at[pl.ds(pl.multiple_of(j * 8, 8), 8), :]

    each(
        2 * groups,
        me,
        lambda j: copy_to(
            rows_of(j), met.at[me], send1.at[j], recv1.at[me], member(j)
        ).start(),
    )
    met[me] = share_ref[pl.ds(pl.multiple_of(me * 8, 8), 8), :]
    each(
        2 * groups,
        me,
        lambda j: copy_to(
            rows_of(j), met.at[j], send1.at[j], recv1.at[j], member(j)
        ).wait_recv(),
    )
    shares = jnp.sum(met[...], axis=0)
    level = noise_level_of(timestep_ref)
    residual, latent, noisy = aux_ref[0:8, :], aux_ref[8:16, :], aux_ref[16:24, :]
    real = noisy - level * (residual + shares[:, :LAT])
    fake = noisy - level * (residual + shares[:, LAT:])
    tiles[group] = jnp.concatenate([fake - real, jnp.abs(latent - real)], axis=1)
    each(
        groups,
        group,
        lambda g: copy_to(
            tiles.at[group], tiles.at[group], send2.at[g], recv2.at[group], peer(g)
        ).start(),
    )
    each(
        groups,
        group,
        lambda g: copy_to(
            tiles.at[g], tiles.at[g], send2.at[g], recv2.at[g], peer(g)
        ).wait_recv(),
    )
    all_tiles = tiles[...]
    gap = jnp.sum(all_tiles, axis=0)
    lane = lax.broadcasted_iota(jnp.int32, gap.shape, 1)
    gap = jnp.where(lane >= LAT, gap, 0.0)
    diff = all_tiles.reshape(tokens, 128)[:, :LAT]
    split = jnp.concatenate(three_parts(diff), axis=1)
    found = lax.dot_general(
        block_ref[...], split, (((0,), (0,)), ((), ())), preferred_element_type=F32
    )
    window[...] = found[:, :LAT] + found[:, LAT : 2 * LAT] + found[:, 2 * LAT :]
    offset = (group % 2) * LAT if grad_rows % 128 else 0

    def fill(p, carry):
        first = window[pl.ds(pl.multiple_of(offset + p * 8, 8), 8), :]
        second = window[pl.ds(pl.multiple_of(offset + grad_rows // 2 + p * 8, 8), 8), :]
        outgoing[p, 0:8, :] = jnp.concatenate([first, second], axis=1)
        outgoing[p, 8:16, :] = gap
        return carry

    lax.fori_loop(0, owners, fill, 0)

    def fill_rest(p, carry):
        outgoing[p, 0:8, :] = jnp.zeros((8, 128), F32)
        outgoing[p, 8:16, :] = gap
        return carry

    lax.fori_loop(owners, seqs, fill_rest, 0)
    each(
        seqs,
        seq,
        lambda p: copy_to(
            outgoing.at[p], arrived.at[seq], send3.at[p], recv3.at[seq], {"seq": p}
        ).start(),
    )
    arrived[seq] = outgoing[seq]
    each(
        seqs,
        seq,
        lambda p: copy_to(
            outgoing.at[p], arrived.at[p], send3.at[p], recv3.at[p], {"seq": p}
        ).wait_recv(),
    )
    sums = jnp.sum(arrived[...], axis=0)
    gap_total = jnp.sum(sums[8:16, :], keepdims=True)
    count = tokens * seqs * LAT
    scale = 1.0 / (gap_total / count + 1e-05)
    diff_ref[...] = scale * diff
    token_scale = float(tokens * seqs) ** -0.5

    @pl.when(seq < owners)
    def _():
        pieces[seq] = (scale * token_scale) * sums[0:8, :]
        each(
            seqs,
            seq,
            lambda p: copy_to(
                pieces.at[seq], pieces.at[seq], send4.at[p], recv4.at[seq], {"seq": p}
            ).start(),
        )

    each(
        owners,
        seq,
        lambda p: copy_to(
            pieces.at[p], pieces.at[p], send4.at[p], recv4.at[p], {"seq": p}
        ).wait_recv(),
    )
    whole = pieces[...].reshape(grad_rows // 2, 128)
    grad_ref[0 : grad_rows // 2, :] = whole[:, :LAT]
    grad_ref[grad_rows // 2 :, :] = whole[:, LAT:]

    each(
        2 * groups,
        me,
        lambda j: copy_to(
            rows_of(j), met.at[me], send1.at[j], recv1.at[me], member(j)
        ).wait_send(),
    )
    each(
        groups,
        group,
        lambda g: copy_to(
            tiles.at[group], tiles.at[group], send2.at[g], recv2.at[group], peer(g)
        ).wait_send(),
    )
    each(
        seqs,
        seq,
        lambda p: copy_to(
            outgoing.at[p], arrived.at[seq], send3.at[p], recv3.at[seq], {"seq": p}
        ).wait_send(),
    )

    @pl.when(seq < owners)
    def _():
        each(
            seqs,
            seq,
            lambda p: copy_to(
                pieces.at[seq], pieces.at[seq], send4.at[p], recv4.at[seq], {"seq": p}
            ).wait_send(),
        )


def local(
    student_hidden_states,
    student_norm_gain,
    student_output_head,
    noise,
    timestep,
    context,
    patch_embedding_input,
    attention_norm_gain,
    query_weight,
    key_weight,
    value_weight,
    adapter_down_weight,
    adapter_up_weight,
    output_weight,
    velocity_head_output,
):
    tokens, width = student_hidden_states.shape
    depth = query_weight.shape[0]
    seqs = lax.axis_size("seq")
    rows_z = seqs // COLUMNS
    groups = lax.axis_size("grp") * lax.axis_size("tp")
    grad_rows = width // groups
    window = grad_rows + LAT if grad_rows % 128 else grad_rows
    vmem = pl.BlockSpec(memory_space=pltpu.VMEM)
    smem = pl.BlockSpec(memory_space=pltpu.SMEM)
    dma = pltpu.SemaphoreType.DMA
    share, aux, block = pl.pallas_call(
        functools.partial(main_kernel, rows_z),
        out_shape=(
            jax.ShapeDtypeStruct((2 * tokens, 2 * LAT), F32),
            jax.ShapeDtypeStruct((24, LAT), F32),
            jax.ShapeDtypeStruct((tokens, window), BF16),
        ),
        in_specs=[smem] + [vmem] * 14,
        out_specs=(vmem, vmem, vmem),
        scratch_shapes=[
            pltpu.VMEM((COLUMNS, rows_z, depth, 512), BF16),
            pltpu.VMEM((depth, 512), BF16),
            pltpu.VMEM((tokens, width), BF16),
            pltpu.VMEM((tokens, width), F32),
            pltpu.VMEM((2, tokens, width), BF16),
            pltpu.VMEM((2, 2 * tokens, HEAD_WIDTH), F32),
            pltpu.VMEM((2, rows_z, 3 * tokens, 128), BF16),
            pltpu.VMEM((2 * rows_z, 4 * tokens, 2 * tokens), F32),
            pltpu.VMEM((4 * tokens, tokens), F32),
            pltpu.VMEM((4 * tokens, tokens), F32),
            pltpu.VMEM((4 * tokens, LAT), F32),
            dma((3 * rows_z,)),
            dma((2 * rows_z,)),
            dma((3 * rows_z,)),
            dma((2 * rows_z,)),
            dma,
            dma,
            dma,
            dma,
        ],
        compiler_params=pltpu.CompilerParams(
            collective_id=0, has_side_effects=True, vmem_limit_bytes=52 * MIB
        ),
    )(
        timestep,
        student_hidden_states,
        student_norm_gain.reshape(1, width),
        student_output_head,
        noise,
        context,
        patch_embedding_input,
        attention_norm_gain.reshape(1, width),
        query_weight,
        key_weight,
        value_weight,
        adapter_down_weight,
        adapter_up_weight,
        output_weight,
        velocity_head_output,
    )
    return pl.pallas_call(
        functools.partial(tail_kernel, rows_z),
        out_shape=(
            jax.ShapeDtypeStruct((tokens, LAT), F32),
            jax.ShapeDtypeStruct((grad_rows, LAT), F32),
        ),
        in_specs=[smem] + [vmem] * 3,
        out_specs=(vmem, vmem),
        scratch_shapes=[
            pltpu.VMEM((2 * groups, 8, 128), F32),
            pltpu.VMEM((groups, 8, 128), F32),
            pltpu.VMEM((window, LAT), F32),
            pltpu.VMEM((seqs, 16, 128), F32),
            pltpu.VMEM((seqs, 16, 128), F32),
            pltpu.VMEM((grad_rows // 16, 8, 128), F32),
            dma((2 * groups,)),
            dma((2 * groups,)),
            dma((groups,)),
            dma((groups,)),
            dma((seqs,)),
            dma((seqs,)),
            dma((seqs,)),
            dma((grad_rows // 16,)),
        ],
        compiler_params=pltpu.CompilerParams(
            collective_id=1, has_side_effects=True, vmem_limit_bytes=32 * MIB
        ),
    )(timestep, share, aux, block)


def solution(mesh):
    heads = P("seq", ("grp", "tp"))
    in_specs = (
        P("seq", None),
        P(),
        P(),
        P("seq", None),
        P(),
        P("seq", None),
        P(),
        P(),
        heads,
        heads,
        heads,
        P("seq", None),
        P(None, ("grp", "tp")),
        P(("grp", "tp"), "seq"),
        P(),
    )
    out_specs = (P("seq", None), P(("grp", "tp"), None))
    return jax.shard_map(local, mesh=mesh, in_specs=in_specs, out_specs=out_specs, check_vma=False)
```

```python
import functools

import jax
import jax.numpy as jnp
from jax import lax
from jax.experimental import pallas as pl
from jax.experimental.pallas import tpu as pltpu
from jax.sharding import PartitionSpec as P

HEAD_WIDTH = 128
LAT = 64
COLUMNS = 4
EPS = 1e-06
F32 = jnp.float32
BF16 = jnp.bfloat16
MIB = 1024 * 1024


def position(rows_z):
    seq = lax.axis_index("seq")
    y, z = seq // rows_z, seq % rows_z
    side = y // 2
    pair = jnp.where(y < 2, y, 3 - y)
    partner = (3 - y) * rows_z + z
    sibling = (y + 1 - 2 * (y % 2)) * rows_z + z
    return seq, y, z, side, pair, partner, sibling


def copy_to(src, dst, send_sem, recv_sem, target):
    return pltpu.make_async_remote_copy(
        src_ref=src,
        dst_ref=dst,
        send_sem=send_sem,
        recv_sem=recv_sem,
        device_id=target,
        device_id_type=pl.DeviceIdType.MESH,
    )


class Chain:
    def __init__(self, unit, send_sem, recv_sem, rows_z):
        self.unit, self.send_sem, self.recv_sem, self.rows_z = unit, send_sem, recv_sem, rows_z
        (self.seq, _, self.z, _, self.pair, _, self.sibling) = position(rows_z)

    def copy(self, pair, row, way, target):
        ref = self.unit(pair, row)
        return copy_to(
            ref,
            ref,
            self.send_sem.at[way * self.rows_z + row],
            self.recv_sem.at[pair * self.rows_z + row],
            {"seq": target},
        )

    def up(self, row):
        return self.copy(self.pair, row, 0, jnp.minimum(self.seq + 1, 4 * self.rows_z - 1))

    def down(self, row):
        return self.copy(self.pair, row, 1, jnp.maximum(self.seq - 1, 0))

    def across(self, row):
        return self.copy(self.pair, row, 2, self.sibling)

    def own(self):
        z = self.z

        @pl.when(z < self.rows_z - 1)
        def _():
            self.up(z).start()

        @pl.when(z > 0)
        def _():
            self.down(z).start()

        self.across(z).start()

    def step(self, t):
        z, last = self.z, self.rows_z - 1

        @pl.when(z - t >= 0)
        def _():
            row = z - t
            self.up(row).wait_recv()

            @pl.when(z < last)
            def _():
                self.up(row).start()

            self.across(row).start()

        @pl.when(z + t <= last)
        def _():
            row = z + t
            self.down(row).wait_recv()

            @pl.when(z > 0)
            def _():
                self.down(row).start()

            self.across(row).start()

    def forward(self):
        def body(t, carry):
            self.step(t)
            return carry

        lax.fori_loop(1, self.rows_z, body, 0)

    def sibling_recv(self):
        def body(row, carry):
            self.copy(1 - self.pair, row, 2, self.sibling).wait_recv()
            return carry

        lax.fori_loop(0, self.rows_z, body, 0)

    def drain(self):
        z, last = self.z, self.rows_z - 1

        def body(row, carry):
            @pl.when(jnp.logical_and(z < last, row <= z))
            def _():
                self.up(row).wait_send()

            @pl.when(jnp.logical_and(z > 0, row >= z))
            def _():
                self.down(row).wait_send()

            self.across(row).wait_send()
            return carry

        lax.fori_loop(0, self.rows_z, body, 0)


def noise_level_of(timestep_ref):
    fraction = jnp.full((1, LAT), timestep_ref[0], jnp.int32).astype(F32) / 1000.0
    return 5.0 * fraction / (1.0 + 4.0 * fraction)


def three_parts(value):
    high = value.astype(BF16)
    rest = value - high.astype(F32)
    middle = rest.astype(BF16)
    low = (rest - middle.astype(F32)).astype(BF16)
    return high, middle, low


def kernel(
    rows_z,
    timestep_ref,
    student_ref,
    student_gain_ref,
    student_head_ref,
    noise_ref,
    context_ref,
    patch_ref,
    gain_ref,
    query_ref,
    key_ref,
    value_ref,
    down_ref,
    up_ref,
    output_ref,
    velocity_ref,
    diff_ref,
    grad_ref,
    qk_weights,
    dv_weights,
    qk_staged,
    vd_staged,
    vd_mail,
    placed,
    fold_out,
    fold_column,
    fold_rows,
    fold_arrived,
    fold_whole,
    act_student,
    hidden,
    act,
    latents,
    first,
    second,
    keys,
    values,
    scores,
    top,
    total,
    mixed,
    share,
    met,
    halves,
    tiles,
    window,
    y_out,
    y_in,
    z_out,
    z_in,
    pieces,
    columns,
    qk_send,
    qk_recv,
    dv_send,
    dv_recv,
    k_send,
    k_recv,
    v_send,
    v_recv,
    one_send,
    one_recv,
):
    seq, y, z, side, pair, partner, sibling = position(rows_z)
    tokens, width = student_ref.shape
    depth = query_ref.shape[0]
    tp_size = lax.axis_size("tp")
    tp = lax.axis_index("tp")
    grp = lax.axis_index("grp")
    groups = lax.axis_size("grp") * tp_size
    group = grp * tp_size + tp
    z_hi, core = grp // 2, grp % 2
    ranks = 2 * tp_size
    rank = core * tp_size + tp
    members = 2 * ranks
    me = side * ranks + rank
    span = width // COLUMNS
    seqs = COLUMNS * rows_z
    here = {"seq": partner}

    def member(k):
        j = (me + k) % members
        column = jnp.where(j // ranks == 0, pair, 3 - pair)
        r = j % ranks
        return j, {
            "grp": z_hi * 2 + r // tp_size,
            "seq": column * rows_z + z,
            "tp": r % tp_size,
        }

    def fellow(k):
        r = (rank + k) % ranks
        return {"grp": z_hi * 2 + r // tp_size, "tp": r % tp_size}

    def in_column(k):
        other = (z + k) % rows_z
        return other, {"seq": y * rows_z + other}

    def in_row(k):
        other = (y + k) % COLUMNS
        return other, {"seq": other * rows_z + z}

    def joined(ref, sem, count):
        part = ref.at[pl.ds(0, count)]
        return copy_to(part, part, one_send.at[sem], one_recv.at[sem], here)

    def send(src, dst, sem, target):
        copy_to(src, dst, one_send.at[sem], one_recv.at[sem], target).start()

    barrier = pltpu.get_barrier_semaphore()

    def greet(target):
        pl.semaphore_signal(
            barrier, inc=1, device_id=target, device_id_type=pl.DeviceIdType.MESH
        )

    for k in range(1, COLUMNS):
        greet(in_row(k)[1])
    for k in range(1, rows_z):
        greet(in_column(k)[1])
    for k in range(1, members):
        if k != ranks:
            greet(member(k)[1])
    greet({"grp": (1 - z_hi) * 2 + core})

    wide = placed.shape[0]
    begin = seq * depth
    offset = begin % 128
    placed[...] = jnp.zeros(placed.shape, BF16)
    placed[pl.ds(pl.multiple_of(offset, 32), depth), :] = output_ref[...]
    folded = jnp.dot(
        velocity_ref[:, pl.ds(pl.multiple_of(begin - offset, 128), wide)],
        placed[...],
        preferred_element_type=F32,
    )
    fold_out[0] = folded[:, :HEAD_WIDTH]
    fold_out[1] = folded[:, HEAD_WIDTH:]
    fold_column[y] = fold_out[side]
    down = down_ref[...].astype(F32).T.astype(BF16)
    own_columns = pl.ds(pl.multiple_of(side * HEAD_WIDTH, HEAD_WIDTH), HEAD_WIDTH)
    other_columns = pl.ds(pl.multiple_of((1 - side) * HEAD_WIDTH, HEAD_WIDTH), HEAD_WIDTH)
    mine = 2 * pair + side
    theirs = 2 * pair + 1 - side
    qk_weights[mine, z, :, 0:128] = query_ref[:, own_columns]
    qk_weights[mine, z, :, 128:256] = key_ref[:, own_columns]
    qk_staged[:, 0:128] = query_ref[:, other_columns]
    qk_staged[:, 128:256] = key_ref[:, other_columns]
    vd_staged[:, 0:128] = value_ref[:, other_columns]
    vd_staged[:, 128:256] = jnp.concatenate([down, down], axis=1)

    pl.semaphore_wait(barrier, 1 + COLUMNS - 1 + rows_z - 1 + members - 2)

    send(qk_staged, qk_weights.at[mine, z], 0, here)
    send(vd_staged, vd_mail, 1, here)
    for k in range(1, COLUMNS):
        other, target = in_row(k)
        send(fold_out.at[other // 2], fold_column.at[y], 2, target)

    chunk = 16

    def student_rows(i, carry):
        rows = pl.ds(pl.multiple_of(i * chunk, chunk), chunk)
        value = student_ref[rows, :].astype(F32)
        scale = lax.rsqrt(jnp.mean(value * value, axis=-1, keepdims=True) + EPS)
        act_student[rows, :] = (value * scale * student_gain_ref[...]).astype(BF16)
        return carry

    lax.fori_loop(0, tokens // chunk, student_rows, 0)

    copy_to(
        qk_staged, qk_weights.at[theirs, z], one_send.at[0], one_recv.at[0], here
    ).wait_recv()
    qk = Chain(lambda p, r: qk_weights.at[pl.ds(2 * p, 2), r], qk_send, qk_recv, rows_z)
    dv = Chain(lambda p, r: dv_weights.at[pl.ds(2 * p, 2), r], dv_send, dv_recv, rows_z)
    qk.own()

    joined(fold_column, 2, COLUMNS - 1).wait_recv()
    fold_rows[...] = jnp.sum(fold_column[...], axis=0).reshape(fold_rows.shape)
    fold_arrived[z] = fold_rows[z]
    for k in range(1, rows_z):
        other, target = in_column(k)
        send(fold_rows.at[other], fold_arrived.at[z], 3, target)

    level = noise_level_of(timestep_ref)
    latent = lax.dot_general(
        act_student[...],
        student_head_ref[...],
        (((1,), (1,)), ((), ())),
        preferred_element_type=F32,
    )
    noise = noise_ref[...].astype(F32).T
    noisy = ((1.0 - level) * latent + level * noise).astype(BF16)
    slab = 512 if width % 512 == 0 else width

    def hidden_columns(i, carry):
        part = pl.ds(pl.multiple_of(i * slab, slab), slab)
        hidden[:, part] = jnp.dot(
            noisy, patch_ref[:, part], preferred_element_type=F32
        ) + context_ref[:, part].astype(F32)
        return carry

    lax.fori_loop(0, width // slab, hidden_columns, 0)

    joined(fold_arrived, 3, rows_z - 1).wait_recv()
    fold_whole[z] = jnp.sum(fold_arrived[...], axis=0)
    for k in range(1, rows_z):
        other, target = in_column(k)
        send(fold_whole.at[z], fold_whole.at[z], 4, target)
    qk.step(1)

    def act_rows(i, carry):
        rows = pl.ds(pl.multiple_of(i * chunk, chunk), chunk)
        value = hidden[rows, :]
        scale = lax.rsqrt(jnp.mean(value * value, axis=-1, keepdims=True) + EPS)
        act[side, rows, :] = (value * scale * gain_ref[...]).astype(BF16)
        return carry

    lax.fori_loop(0, tokens // chunk, act_rows, 0)
    send(act.at[side], act.at[side], 5, here)

    joined(fold_whole, 4, rows_z - 1).wait_recv()
    whole = fold_whole[...].reshape(LAT, HEAD_WIDTH)
    high = whole.astype(BF16)
    rest = (whole - high.astype(F32)).astype(BF16)
    split = jnp.concatenate([high, rest], axis=0)
    copy_to(vd_staged, vd_mail, one_send.at[1], one_recv.at[1], here).wait_recv()
    for place, value, lower in (
        (mine, value_ref[:, own_columns], down),
        (theirs, vd_mail[:, 0:128], vd_mail[:, 128 : 128 + LAT]),
    ):
        moved = lax.dot_general(
            value, split, (((1,), (1,)), ((), ())), preferred_element_type=F32
        )
        moved = (moved[:, :LAT] + moved[:, LAT:]).astype(BF16)
        dv_weights[place, z] = jnp.concatenate([lower, moved], axis=1)
    dv.own()
    qk.step(2)

    taken = pl.ds(pl.multiple_of(rank * 16, 16), 16)
    latents[0] = latent
    latents[1] = noisy.astype(F32)
    parts = jnp.concatenate(three_parts(hidden[taken, :]), axis=0)
    residual = lax.dot_general(
        parts, velocity_ref[...], (((1,), (1,)), ((), ())), preferred_element_type=F32
    )
    residual = residual[0:16] + residual[16:32] + residual[32:48]

    def both_steps(t, carry):
        dv.step(t)
        qk.step(t + 2)
        return carry

    lax.fori_loop(1, rows_z, both_steps, 0)
    copy_to(
        act.at[1 - side], act.at[1 - side], one_send.at[5], one_recv.at[5], here
    ).wait_recv()

    def project(place, column, fresh):
        part = pl.ds(pl.multiple_of(column * span, span), span)
        rows = act[:, :, part].reshape(2 * tokens, span)
        one = jnp.dot(
            rows, qk_weights[place].reshape(span, 256), preferred_element_type=F32
        )
        two = jnp.dot(
            rows, dv_weights[place].reshape(span, 128), preferred_element_type=F32
        )
        first[...] = one if fresh else first[...] + one
        second[...] = two if fresh else second[...] + two

    project(2 * pair, pair, True)
    project(2 * pair + 1, 3 - pair, False)
    qk.sibling_recv()
    dv.sibling_recv()
    project(2 - 2 * pair, 1 - pair, False)
    project(3 - 2 * pair, 2 + pair, False)

    keys[pair, z] = first[:, 128:256].astype(BF16)
    k_chain = Chain(lambda p, r: keys.at[p, r], k_send, k_recv, rows_z)
    v_chain = Chain(lambda p, r: values.at[p, r], v_send, v_recv, rows_z)
    k_chain.own()
    moved = second[:, LAT:].astype(BF16)
    values[pair, z] = jnp.concatenate([moved[:tokens], moved[tokens:]], axis=1)
    v_chain.own()

    low = second[:, :LAT].astype(BF16)
    plain = first[:, 0:128]
    fake = plain + jnp.dot(low, up_ref[:, own_columns], preferred_element_type=F32)
    asked = jnp.concatenate([plain, fake], axis=0).astype(BF16)
    top[...] = jnp.full(top.shape, -1e30, F32)
    factor = HEAD_WIDTH**-0.5

    def score_unit(p, r):
        found = (
            lax.dot_general(
                asked, keys[p, r], (((1,), (1,)), ((), ())), preferred_element_type=F32
            )
            * factor
        )
        scores[p * rows_z + r] = found
        top[...] = jnp.maximum(
            top[...], jnp.maximum(found[:, :tokens], found[:, tokens:])
        )

    def kv_steps(t, carry):
        k_chain.step(t)
        v_chain.step(t)

        def way(d, carry):
            r = z + (1 - 2 * d) * (t - 1)
            fits = jnp.logical_and(r >= 0, r < rows_z)

            @pl.when(jnp.logical_and(fits, jnp.logical_or(t > 1, d == 0)))
            def _():
                score_unit(pair, r)

            return carry

        lax.fori_loop(0, 2, way, 0)
        return carry

    lax.fori_loop(1, rows_z + 1, kv_steps, 0)

    def from_sibling(r, carry):
        k_chain.copy(1 - pair, r, 2, sibling).wait_recv()
        score_unit(1 - pair, r)
        return carry

    lax.fori_loop(0, rows_z, from_sibling, 0)
    v_chain.sibling_recv()
    peak = jnp.max(top[...], axis=-1, keepdims=True)
    top[...] = jnp.broadcast_to(peak, top.shape)
    total[...] = jnp.zeros(total.shape, F32)
    mixed[...] = jnp.zeros(mixed.shape, F32)

    def mix_unit(u, carry):
        shift = top[...]
        left = jnp.exp(scores[u, :, 0:tokens] - shift)
        right = jnp.exp(scores[u, :, tokens : 2 * tokens] - shift)
        total[...] += left + right
        packed = values[u // rows_z, u % rows_z]
        stacked = jnp.concatenate([packed[:, :LAT], packed[:, LAT:]], axis=0)
        mixed[...] += jnp.dot(
            jnp.concatenate([left, right], axis=1).astype(BF16),
            stacked,
            preferred_element_type=F32,
        )
        return carry

    lax.fori_loop(0, 2 * rows_z, mix_unit, 0)
    attended = mixed[...] / jnp.sum(total[...], axis=-1, keepdims=True)
    share[...] = jnp.concatenate(
        [attended[: 2 * tokens], attended[2 * tokens :]], axis=1
    ).reshape(share.shape)

    for k in range(1, members):
        j, target = member(k)
        send(share.at[j], met.at[me], 6, target)
    met[me] = share[me]
    joined(met, 6, members - 1).wait_recv()
    halves[0] = jnp.sum(met[...], axis=0)
    send(halves.at[0], halves.at[1], 7, {"grp": (1 - z_hi) * 2 + core})
    joined(halves, 7, 1).wait_recv()
    shares = halves[0] + halves[1]
    taken_latent = latents[0, taken, :]
    taken_noisy = latents[1, taken, :]
    real = taken_noisy - level * (residual + shares[:, :LAT])
    fake_pred = taken_noisy - level * (residual + shares[:, LAT:])
    tiles[rank] = jnp.concatenate(
        [fake_pred - real, jnp.abs(taken_latent - real)], axis=1
    )
    for k in range(1, ranks):
        send(tiles.at[rank], tiles.at[rank], 8, fellow(k))
    joined(tiles, 8, ranks - 1).wait_recv()
    all_tiles = tiles[...]
    gap = jnp.sum(all_tiles, axis=0)
    gap = gap[0:8] + gap[8:16]
    lane = lax.broadcasted_iota(jnp.int32, gap.shape, 1)
    gap = jnp.where(lane >= LAT, gap, 0.0)
    diff = all_tiles.reshape(tokens, 128)[:, :LAT]

    grad_rows = grad_ref.shape[0]
    start, skip = group * grad_rows, 0
    if grad_rows % 128:
        skip = (group % 2) * LAT
        start = start - skip
    found = lax.dot_general(
        act_student[:, pl.ds(pl.multiple_of(start, 128), window.shape[0])],
        jnp.concatenate(three_parts(diff), axis=1),
        (((0,), (0,)), ((), ())),
        preferred_element_type=F32,
    )
    window[...] = found[:, :LAT] + found[:, LAT : 2 * LAT] + found[:, 2 * LAT :]
    quarter = grad_rows // 8
    for column in range(COLUMNS):
        low_rows = pl.multiple_of(skip + column * quarter, 8)
        high_rows = pl.multiple_of(skip + grad_rows // 2 + column * quarter, 8)
        y_out[column, 0:quarter, :] = jnp.concatenate(
            [window[pl.ds(low_rows, quarter), :], window[pl.ds(high_rows, quarter), :]],
            axis=1,
        )
        y_out[column, quarter : quarter + 8, :] = gap
    for k in range(1, COLUMNS):
        other, target = in_row(k)
        send(y_out.at[other], y_in.at[y], 9, target)
    y_in[y] = y_out[y]
    joined(y_in, 9, COLUMNS - 1).wait_recv()
    sums = jnp.sum(y_in[...], axis=0)
    owners = quarter // 8
    for r in range(rows_z):
        z_out[r, 0:8, :] = (
            sums[8 * r : 8 * r + 8] if r < owners else jnp.zeros((8, 128), F32)
        )
        z_out[r, 8:16, :] = sums[quarter:]
    for k in range(1, rows_z):
        other, target = in_column(k)
        send(z_out.at[other], z_in.at[z], 10, target)
    z_in[z] = z_out[z]
    joined(z_in, 10, rows_z - 1).wait_recv()
    sums = jnp.sum(z_in[...], axis=0)
    gap_total = jnp.sum(sums[8:16, :], keepdims=True)
    scale = 1.0 / (gap_total / (tokens * seqs * LAT) + 1e-05)
    token_scale = float(tokens * seqs) ** -0.5

    @pl.when(z < owners)
    def _():
        pieces[z] = (scale * token_scale) * sums[0:8, :]
        for k in range(1, rows_z):
            _, target = in_column(k)
            send(pieces.at[z], pieces.at[z], 11, target)
        if owners > 1:
            joined(pieces, 11, owners - 1).wait_recv()

    if owners < rows_z:

        @pl.when(z >= owners)
        def _():
            joined(pieces, 11, owners).wait_recv()

    columns[y] = pieces[...].reshape(quarter, 128)
    for k in range(1, COLUMNS):
        _, target = in_row(k)
        send(columns.at[y], columns.at[y], 12, target)
    diff_ref[...] = scale * diff
    joined(columns, 12, COLUMNS - 1).wait_recv()
    complete = columns[...].reshape(grad_rows // 2, 128)
    grad_ref[0 : grad_rows // 2, :] = complete[:, :LAT]
    grad_ref[grad_rows // 2 :, :] = complete[:, LAT:]

    copy_to(qk_staged, qk_staged, one_send.at[0], one_recv.at[0], here).wait_send()
    copy_to(vd_staged, vd_mail, one_send.at[1], one_recv.at[1], here).wait_send()
    joined(fold_column, 2, COLUMNS - 1).wait_send()
    joined(fold_rows, 3, rows_z - 1).wait_send()
    joined(fold_whole, 4, rows_z - 1).wait_send()
    joined(act, 5, 1).wait_send()
    joined(share, 6, members - 1).wait_send()
    joined(halves, 7, 1).wait_send()
    joined(tiles, 8, ranks - 1).wait_send()
    joined(y_out, 9, COLUMNS - 1).wait_send()
    joined(z_out, 10, rows_z - 1).wait_send()

    @pl.when(z < owners)
    def _():
        for _ in range(1, rows_z):
            joined(pieces, 11, 1).wait_send()

    joined(columns, 12, COLUMNS - 1).wait_send()
    qk.drain()
    dv.drain()
    k_chain.drain()
    v_chain.drain()


def local(
    student_hidden_states,
    student_norm_gain,
    student_output_head,
    noise,
    timestep,
    context,
    patch_embedding_input,
    attention_norm_gain,
    query_weight,
    key_weight,
    value_weight,
    adapter_down_weight,
    adapter_up_weight,
    output_weight,
    velocity_head_output,
):
    tokens, width = student_hidden_states.shape
    depth = query_weight.shape[0]
    seqs = lax.axis_size("seq")
    rows_z = seqs // COLUMNS
    groups = lax.axis_size("grp") * lax.axis_size("tp")
    ranks = 2 * lax.axis_size("tp")
    grad_rows = width // groups
    window = grad_rows + LAT if grad_rows % 128 else grad_rows
    quarter = grad_rows // 8
    vmem = pl.BlockSpec(memory_space=pltpu.VMEM)
    smem = pl.BlockSpec(memory_space=pltpu.SMEM)
    dma = pltpu.SemaphoreType.DMA
    chain = [dma((3 * rows_z,)), dma((2 * rows_z,))]
    return pl.pallas_call(
        functools.partial(kernel, rows_z),
        out_shape=(
            jax.ShapeDtypeStruct((tokens, LAT), F32),
            jax.ShapeDtypeStruct((grad_rows, LAT), F32),
        ),
        in_specs=[smem] + [vmem] * 14,
        out_specs=(vmem, vmem),
        scratch_shapes=[
            pltpu.VMEM((COLUMNS, rows_z, depth, 256), BF16),
            pltpu.VMEM((COLUMNS, rows_z, depth, 128), BF16),
            pltpu.VMEM((depth, 256), BF16),
            pltpu.VMEM((depth, 256), BF16),
            pltpu.VMEM((depth, 256), BF16),
            pltpu.VMEM((256 if depth % 128 else depth, 256), BF16),
            pltpu.VMEM((2, LAT, HEAD_WIDTH), F32),
            pltpu.VMEM((COLUMNS, LAT, HEAD_WIDTH), F32),
            pltpu.VMEM((rows_z, LAT // rows_z, HEAD_WIDTH), F32),
            pltpu.VMEM((rows_z, LAT // rows_z, HEAD_WIDTH), F32),
            pltpu.VMEM((rows_z, LAT // rows_z, HEAD_WIDTH), F32),
            pltpu.VMEM((tokens, width), BF16),
            pltpu.VMEM((tokens, width), F32),
            pltpu.VMEM((2, tokens, width), BF16),
            pltpu.VMEM((2, tokens, LAT), F32),
            pltpu.VMEM((2 * tokens, 256), F32),
            pltpu.VMEM((2 * tokens, 128), F32),
            pltpu.VMEM((2, rows_z, 2 * tokens, HEAD_WIDTH), BF16),
            pltpu.VMEM((2, rows_z, tokens, 128), BF16),
            pltpu.VMEM((2 * rows_z, 4 * tokens, 2 * tokens), F32),
            pltpu.VMEM((4 * tokens, tokens), F32),
            pltpu.VMEM((4 * tokens, tokens), F32),
            pltpu.VMEM((4 * tokens, LAT), F32),
            pltpu.VMEM((2 * ranks, 16, 128), F32),
            pltpu.VMEM((2 * ranks, 16, 128), F32),
            pltpu.VMEM((2, 16, 128), F32),
            pltpu.VMEM((ranks, 16, 128), F32),
            pltpu.VMEM((window, LAT), F32),
            pltpu.VMEM((COLUMNS, quarter + 8, 128), F32),
            pltpu.VMEM((COLUMNS, quarter + 8, 128), F32),
            pltpu.VMEM((rows_z, 16, 128), F32),
            pltpu.VMEM((rows_z, 16, 128), F32),
            pltpu.VMEM((quarter // 8, 8, 128), F32),
            pltpu.VMEM((COLUMNS, quarter, 128), F32),
        ]
        + chain * 4
        + [dma((13,)), dma((13,))],
        compiler_params=pltpu.CompilerParams(
            collective_id=0, has_side_effects=True, vmem_limit_bytes=52 * MIB
        ),
    )(
        timestep,
        student_hidden_states,
        student_norm_gain.reshape(1, width),
        student_output_head.T,
        noise.T,
        context,
        patch_embedding_input,
        attention_norm_gain.reshape(1, width),
        query_weight,
        key_weight,
        value_weight,
        adapter_down_weight.T,
        adapter_up_weight,
        output_weight.T,
        velocity_head_output.T,
    )


def solution(mesh):
    heads = P("seq", ("grp", "tp"))
    in_specs = (
        P("seq", None),
        P(),
        P(),
        P("seq", None),
        P(),
        P("seq", None),
        P(),
        P(),
        heads,
        heads,
        heads,
        P("seq", None),
        P(None, ("grp", "tp")),
        P(("grp", "tp"), "seq"),
        P(),
    )
    out_specs = (P("seq", None), P(("grp", "tp"), None))
    return jax.shard_map(local, mesh=mesh, in_specs=in_specs, out_specs=out_specs, check_vma=False)
```

```python
import functools

import jax
import jax.numpy as jnp
from jax import lax
from jax.experimental import pallas as pl
from jax.experimental.pallas import tpu as pltpu
from jax.sharding import PartitionSpec as P

HEAD_WIDTH = 128
LAT = 64
COLUMNS = 4
EPS = 1e-06
F32 = jnp.float32
BF16 = jnp.bfloat16
MIB = 1024 * 1024


def position(rows_z):
    seq = lax.axis_index("seq")
    y, z = seq // rows_z, seq % rows_z
    side = y // 2
    pair = jnp.where(y < 2, y, 3 - y)
    partner = (3 - y) * rows_z + z
    sibling = (y + 1 - 2 * (y % 2)) * rows_z + z
    return seq, y, z, side, pair, partner, sibling


def copy_to(src, dst, send_sem, recv_sem, target):
    return pltpu.make_async_remote_copy(
        src_ref=src,
        dst_ref=dst,
        send_sem=send_sem,
        recv_sem=recv_sem,
        device_id=target,
        device_id_type=pl.DeviceIdType.MESH,
    )


class Chain:
    def __init__(self, unit, send_sem, recv_sem, rows_z):
        self.unit, self.send_sem, self.recv_sem, self.rows_z = unit, send_sem, recv_sem, rows_z
        (self.seq, _, self.z, _, self.pair, _, self.sibling) = position(rows_z)

    def copy(self, pair, row, way, target):
        ref = self.unit(pair, row)
        return copy_to(
            ref,
            ref,
            self.send_sem.at[way * self.rows_z + row],
            self.recv_sem.at[pair * self.rows_z + row],
            {"seq": target},
        )

    def up(self, row):
        return self.copy(self.pair, row, 0, jnp.minimum(self.seq + 1, 4 * self.rows_z - 1))

    def down(self, row):
        return self.copy(self.pair, row, 1, jnp.maximum(self.seq - 1, 0))

    def across(self, row):
        return self.copy(self.pair, row, 2, self.sibling)

    def own(self):
        z = self.z

        @pl.when(z < self.rows_z - 1)
        def _():
            self.up(z).start()

        @pl.when(z > 0)
        def _():
            self.down(z).start()

        self.across(z).start()

    def step(self, t):
        z, last = self.z, self.rows_z - 1

        @pl.when(z - t >= 0)
        def _():
            row = z - t
            self.up(row).wait_recv()

            @pl.when(z < last)
            def _():
                self.up(row).start()

            self.across(row).start()

        @pl.when(z + t <= last)
        def _():
            row = z + t
            self.down(row).wait_recv()

            @pl.when(z > 0)
            def _():
                self.down(row).start()

            self.across(row).start()

    def forward(self):
        def body(t, carry):
            self.step(t)
            return carry

        lax.fori_loop(1, self.rows_z, body, 0)

    def sibling_recv(self):
        def body(row, carry):
            self.copy(1 - self.pair, row, 2, self.sibling).wait_recv()
            return carry

        lax.fori_loop(0, self.rows_z, body, 0)

    def drain(self):
        z, last = self.z, self.rows_z - 1

        def body(row, carry):
            @pl.when(jnp.logical_and(z < last, row <= z))
            def _():
                self.up(row).wait_send()

            @pl.when(jnp.logical_and(z > 0, row >= z))
            def _():
                self.down(row).wait_send()

            self.across(row).wait_send()
            return carry

        lax.fori_loop(0, self.rows_z, body, 0)


def noise_level_of(timestep_ref):
    fraction = jnp.full((1, LAT), timestep_ref[0], jnp.int32).astype(F32) / 1000.0
    return 5.0 * fraction / (1.0 + 4.0 * fraction)


def three_parts(value):
    high = value.astype(BF16)
    rest = value - high.astype(F32)
    middle = rest.astype(BF16)
    low = (rest - middle.astype(F32)).astype(BF16)
    return high, middle, low


def kernel(
    rows_z,
    timestep_ref,
    student_hbm,
    student_gain_hbm,
    student_head_hbm,
    noise_hbm,
    context_hbm,
    patch_hbm,
    gain_hbm,
    query_hbm,
    key_hbm,
    value_hbm,
    down_hbm,
    up_hbm,
    output_hbm,
    velocity_hbm,
    diff_ref,
    grad_ref,
    student_ref,
    student_gain_ref,
    student_head_ref,
    noise_ref,
    context_ref,
    patch_ref,
    gain_ref,
    up_ref,
    output_ref,
    velocity_ref,
    down_own,
    down_mail,
    value_own,
    value_mail,
    k_weights,
    q_weights,
    v_weights,
    down_weights,
    placed,
    fold_out,
    fold_column,
    fold_rows,
    fold_arrived,
    fold_whole,
    act_student,
    hidden,
    act,
    latents,
    k_product,
    q_product,
    v_product,
    low_product,
    keys,
    values,
    scores,
    top,
    total,
    mixed,
    share,
    met,
    halves,
    tiles,
    window,
    y_out,
    y_in,
    z_out,
    z_in,
    pieces,
    columns,
    kw_send,
    kw_recv,
    qw_send,
    qw_recv,
    vw_send,
    vw_recv,
    dw_send,
    dw_recv,
    ka_send,
    ka_recv,
    kb_send,
    kb_recv,
    v_send,
    v_recv,
    one_send,
    one_recv,
    load_sem,
):
    seq, y, z, side, pair, partner, sibling = position(rows_z)
    tokens, width = student_ref.shape
    depth = query_hbm.shape[0]
    tp_size = lax.axis_size("tp")
    tp = lax.axis_index("tp")
    grp = lax.axis_index("grp")
    groups = lax.axis_size("grp") * tp_size
    group = grp * tp_size + tp
    z_hi, core = grp // 2, grp % 2
    ranks = 2 * tp_size
    rank = core * tp_size + tp
    members = 2 * ranks
    me = side * ranks + rank
    span = width // COLUMNS
    seqs = COLUMNS * rows_z
    here = {"seq": partner}

    def member(k):
        j = (me + k) % members
        column = jnp.where(j // ranks == 0, pair, 3 - pair)
        r = j % ranks
        return j, {
            "grp": z_hi * 2 + r // tp_size,
            "seq": column * rows_z + z,
            "tp": r % tp_size,
        }

    def fellow(k):
        r = (rank + k) % ranks
        return {"grp": z_hi * 2 + r // tp_size, "tp": r % tp_size}

    def in_column(k):
        other = (z + k) % rows_z
        return other, {"seq": y * rows_z + other}

    def in_row(k):
        other = (y + k) % COLUMNS
        return other, {"seq": other * rows_z + z}

    def joined(ref, sem, count):
        part = ref.at[pl.ds(0, count)]
        return copy_to(part, part, one_send.at[sem], one_recv.at[sem], here)

    def send(src, dst, sem, target):
        copy_to(src, dst, one_send.at[sem], one_recv.at[sem], target).start()

    own_columns = pl.ds(pl.multiple_of(side * HEAD_WIDTH, HEAD_WIDTH), HEAD_WIDTH)
    other_columns = pl.ds(pl.multiple_of((1 - side) * HEAD_WIDTH, HEAD_WIDTH), HEAD_WIDTH)
    mine = 2 * pair + side
    theirs = 2 * pair + 1 - side
    sources = (
        (output_hbm, output_ref),
        (velocity_hbm, velocity_ref),
        (student_hbm, student_ref),
        (student_gain_hbm, student_gain_ref),
        (key_hbm.at[:, own_columns], k_weights.at[mine, z]),
        (query_hbm.at[:, own_columns], q_weights.at[mine, z]),
        (student_head_hbm, student_head_ref),
        (noise_hbm, noise_ref),
        (patch_hbm, patch_ref),
        (context_hbm, context_ref),
        (gain_hbm, gain_ref),
        (value_hbm.at[:, own_columns], value_own),
        (down_hbm, down_own),
        (up_hbm, up_ref),
    )
    loads = [
        pltpu.make_async_copy(src, dst, load_sem.at[i]) for i, (src, dst) in enumerate(sources)
    ]
    for load in loads:
        load.start()

    barrier = pltpu.get_barrier_semaphore()

    def greet(target):
        pl.semaphore_signal(
            barrier, inc=1, device_id=target, device_id_type=pl.DeviceIdType.MESH
        )

    for k in range(1, COLUMNS):
        greet(in_row(k)[1])
    for k in range(1, rows_z):
        greet(in_column(k)[1])
    for k in range(1, members):
        if k != ranks:
            greet(member(k)[1])
    greet({"grp": (1 - z_hi) * 2 + core})

    loads[0].wait()
    loads[1].wait()
    wide = placed.shape[0]
    begin = seq * depth
    offset = begin % 128
    placed[...] = jnp.zeros(placed.shape, BF16)
    placed[pl.ds(pl.multiple_of(offset, 32), depth), :] = output_ref[...]
    folded = jnp.dot(
        velocity_ref[:, pl.ds(pl.multiple_of(begin - offset, 128), wide)],
        placed[...],
        preferred_element_type=F32,
    )
    fold_out[0] = folded[:, :HEAD_WIDTH]
    fold_out[1] = folded[:, HEAD_WIDTH:]
    fold_column[y] = fold_out[side]

    pl.semaphore_wait(barrier, 1 + COLUMNS - 1 + rows_z - 1 + members - 2)

    send(key_hbm.at[:, other_columns], k_weights.at[mine, z], 0, here)
    for k in range(1, COLUMNS):
        other, target = in_row(k)
        send(fold_out.at[other // 2], fold_column.at[y], 2, target)
    send(query_hbm.at[:, other_columns], q_weights.at[mine, z], 13, here)
    send(value_hbm.at[:, other_columns], value_mail, 1, here)
    send(down_hbm, down_mail, 14, here)
    loads[2].wait()
    loads[3].wait()

    chunk = 16

    def student_rows(i, carry):
        rows = pl.ds(pl.multiple_of(i * chunk, chunk), chunk)
        value = student_ref[rows, :].astype(F32)
        scale = lax.rsqrt(jnp.mean(value * value, axis=-1, keepdims=True) + EPS)
        act_student[rows, :] = (value * scale * student_gain_ref[...]).astype(BF16)
        return carry

    lax.fori_loop(0, tokens // chunk, student_rows, 0)

    def came(src, dst, sem):
        copy_to(src, dst, one_send.at[sem], one_recv.at[sem], here).wait_recv()

    def two_slots(ref):
        return lambda p, r: ref.at[pl.ds(2 * p, 2), r]

    kw = Chain(two_slots(k_weights), kw_send, kw_recv, rows_z)
    qw = Chain(two_slots(q_weights), qw_send, qw_recv, rows_z)
    vw = Chain(lambda p, r: v_weights.at[p, r], vw_send, vw_recv, rows_z)
    dw = Chain(lambda p, r: down_weights.at[p, r], dw_send, dw_recv, rows_z)
    loads[4].wait()
    came(key_hbm.at[:, other_columns], k_weights.at[theirs, z], 0)
    kw.own()

    joined(fold_column, 2, COLUMNS - 1).wait_recv()
    fold_rows[...] = jnp.sum(fold_column[...], axis=0).reshape(fold_rows.shape)
    fold_arrived[z] = fold_rows[z]
    for k in range(1, rows_z):
        other, target = in_column(k)
        send(fold_rows.at[other], fold_arrived.at[z], 3, target)
    loads[5].wait()
    came(query_hbm.at[:, other_columns], q_weights.at[theirs, z], 13)
    qw.own()
    loads[6].wait()
    loads[7].wait()

    level = noise_level_of(timestep_ref)
    latent = lax.dot_general(
        act_student[...],
        student_head_ref[...],
        (((1,), (1,)), ((), ())),
        preferred_element_type=F32,
    )
    noise = noise_ref[...].astype(F32).T
    noisy = ((1.0 - level) * latent + level * noise).astype(BF16)
    loads[8].wait()
    loads[9].wait()
    slab = 512 if width % 512 == 0 else width

    def hidden_columns(i, carry):
        part = pl.ds(pl.multiple_of(i * slab, slab), slab)
        hidden[:, part] = jnp.dot(
            noisy, patch_ref[:, part], preferred_element_type=F32
        ) + context_ref[:, part].astype(F32)
        return carry

    lax.fori_loop(0, width // slab, hidden_columns, 0)

    kw.step(1)
    joined(fold_arrived, 3, rows_z - 1).wait_recv()
    fold_whole[z] = jnp.sum(fold_arrived[...], axis=0)
    for k in range(1, rows_z):
        other, target = in_column(k)
        send(fold_whole.at[z], fold_whole.at[z], 4, target)
    loads[10].wait()

    def act_rows(i, carry):
        rows = pl.ds(pl.multiple_of(i * chunk, chunk), chunk)
        value = hidden[rows, :]
        scale = lax.rsqrt(jnp.mean(value * value, axis=-1, keepdims=True) + EPS)
        act[side, rows, :] = (value * scale * gain_ref[...]).astype(BF16)
        return carry

    lax.fori_loop(0, tokens // chunk, act_rows, 0)
    half = tokens // 2
    this_half = pl.ds(pl.multiple_of(core * half, half), half)
    that_half = pl.ds(pl.multiple_of((1 - core) * half, half), half)
    send(act.at[side, this_half], act.at[side, this_half], 5, here)
    qw.step(1)
    kw.step(2)

    joined(fold_whole, 4, rows_z - 1).wait_recv()
    whole = fold_whole[...].reshape(LAT, HEAD_WIDTH)
    high = whole.astype(BF16)
    rest = (whole - high.astype(F32)).astype(BF16)
    split = jnp.concatenate([high, rest], axis=0)
    loads[11].wait()
    came(value_hbm.at[:, other_columns], value_mail, 1)

    def fold_value(ref):
        moved = lax.dot_general(
            ref[...], split, (((1,), (1,)), ((), ())), preferred_element_type=F32
        )
        return moved[:, :LAT] + moved[:, LAT:]

    def in_order(own, other):
        lower = jnp.where(side == 0, own, other)
        upper = jnp.where(side == 0, other, own)
        return jnp.concatenate([lower, upper], axis=1).astype(BF16)

    v_weights[pair, z] = in_order(fold_value(value_own), fold_value(value_mail))
    vw.own()
    loads[12].wait()
    came(down_hbm, down_mail, 14)
    down_weights[pair, z] = in_order(
        down_own[...].astype(F32).T, down_mail[...].astype(F32).T
    )
    dw.own()
    qw.step(2)

    taken = pl.ds(pl.multiple_of(rank * 16, 16), 16)
    latents[0] = latent
    latents[1] = noisy.astype(F32)
    parts = jnp.concatenate(three_parts(hidden[taken, :]), axis=0)
    residual = lax.dot_general(
        parts, velocity_ref[...], (((1,), (1,)), ((), ())), preferred_element_type=F32
    )
    residual = residual[0:16] + residual[16:32] + residual[32:48]

    def weight_steps(t, carry):
        kw.step(t + 2)
        vw.step(t)
        qw.step(t + 2)
        dw.step(t)
        return carry

    middle = min(4, rows_z)
    lax.fori_loop(1, middle, weight_steps, 0)
    came(act.at[1 - side, this_half], act.at[1 - side, this_half], 5)
    core_mate = {"grp": grp + 1 - 2 * core}
    send(act.at[1 - side, this_half], act.at[1 - side, this_half], 15, core_mate)
    lax.fori_loop(middle, rows_z, weight_steps, 0)
    came(act.at[1 - side, that_half], act.at[1 - side, that_half], 15)

    def rows_at(column):
        part = pl.ds(pl.multiple_of(column * span, span), span)
        return act[:, :, part].reshape(2 * tokens, span)

    def project(weights, p):
        lower = jnp.dot(
            rows_at(p), weights[2 * p].reshape(span, 128), preferred_element_type=F32
        )
        upper = jnp.dot(
            rows_at(3 - p), weights[2 * p + 1].reshape(span, 128), preferred_element_type=F32
        )
        return lower + upper

    def project_packed(weights, p):
        packed = weights[p].reshape(span, 128)
        lower = jnp.dot(rows_at(p), packed, preferred_element_type=F32)
        upper = jnp.dot(rows_at(3 - p), packed, preferred_element_type=F32)
        return lower[:, :LAT] + upper[:, LAT:]

    k_product[...] = project(k_weights, pair)
    kw.sibling_recv()
    keys[pair, z] = (k_product[...] + project(k_weights, 1 - pair)).astype(BF16)
    ka = Chain(lambda p, r: keys.at[p, r, pl.ds(0, tokens)], ka_send, ka_recv, rows_z)
    kb = Chain(lambda p, r: keys.at[p, r, pl.ds(tokens, tokens)], kb_send, kb_recv, rows_z)
    vs = Chain(lambda p, r: values.at[p, r], v_send, v_recv, rows_z)
    ka.own()
    kb.own()
    v_product[...] = project_packed(v_weights, pair)
    vw.sibling_recv()
    moved = (v_product[...] + project_packed(v_weights, 1 - pair)).astype(BF16)
    values[pair, z] = jnp.concatenate([moved[:tokens], moved[tokens:]], axis=1)
    vs.own()
    q_product[...] = project(q_weights, pair)
    low_product[...] = project_packed(down_weights, pair)
    qw.sibling_recv()
    plain = q_product[...] + project(q_weights, 1 - pair)
    dw.sibling_recv()
    low = (low_product[...] + project_packed(down_weights, 1 - pair)).astype(BF16)
    loads[13].wait()
    fake = plain + jnp.dot(low, up_ref[:, own_columns], preferred_element_type=F32)
    asked = jnp.concatenate([plain, fake], axis=0).astype(BF16)
    top[...] = jnp.full(top.shape, -1e30, F32)
    factor = HEAD_WIDTH**-0.5

    def score_unit(p, r):
        found = (
            lax.dot_general(
                asked, keys[p, r], (((1,), (1,)), ((), ())), preferred_element_type=F32
            )
            * factor
        )
        scores[p * rows_z + r] = found
        top[...] = jnp.maximum(
            top[...], jnp.maximum(found[:, :tokens], found[:, tokens:])
        )

    def kv_steps(t, carry):
        ka.step(t)
        kb.step(t)
        vs.step(t)

        def way(d, carry):
            r = z + (1 - 2 * d) * (t - 1)
            fits = jnp.logical_and(r >= 0, r < rows_z)

            @pl.when(jnp.logical_and(fits, jnp.logical_or(t > 1, d == 0)))
            def _():
                score_unit(pair, r)

            return carry

        lax.fori_loop(0, 2, way, 0)
        return carry

    lax.fori_loop(1, rows_z + 1, kv_steps, 0)

    def from_sibling(r, carry):
        ka.copy(1 - pair, r, 2, sibling).wait_recv()
        kb.copy(1 - pair, r, 2, sibling).wait_recv()
        score_unit(1 - pair, r)
        return carry

    lax.fori_loop(0, rows_z, from_sibling, 0)
    vs.sibling_recv()
    peak = jnp.max(top[...], axis=-1, keepdims=True)
    top[...] = jnp.broadcast_to(peak, top.shape)
    total[...] = jnp.zeros(total.shape, F32)
    mixed[...] = jnp.zeros(mixed.shape, F32)

    def mix_unit(u, carry):
        shift = top[...]
        left = jnp.exp(scores[u, :, 0:tokens] - shift)
        right = jnp.exp(scores[u, :, tokens : 2 * tokens] - shift)
        total[...] += left + right
        packed = values[u // rows_z, u % rows_z]
        stacked = jnp.concatenate([packed[:, :LAT], packed[:, LAT:]], axis=0)
        mixed[...] += jnp.dot(
            jnp.concatenate([left, right], axis=1).astype(BF16),
            stacked,
            preferred_element_type=F32,
        )
        return carry

    lax.fori_loop(0, 2 * rows_z, mix_unit, 0)
    attended = mixed[...] / jnp.sum(total[...], axis=-1, keepdims=True)
    share[...] = jnp.concatenate(
        [attended[: 2 * tokens], attended[2 * tokens :]], axis=1
    ).reshape(share.shape)

    for k in range(1, members):
        j, target = member(k)
        send(share.at[j], met.at[me], 6, target)
    met[me] = share[me]
    joined(met, 6, members - 1).wait_recv()
    halves[0] = jnp.sum(met[...], axis=0)
    send(halves.at[0], halves.at[1], 7, {"grp": (1 - z_hi) * 2 + core})
    joined(halves, 7, 1).wait_recv()
    shares = halves[0] + halves[1]
    taken_latent = latents[0, taken, :]
    taken_noisy = latents[1, taken, :]
    real = taken_noisy - level * (residual + shares[:, :LAT])
    fake_pred = taken_noisy - level * (residual + shares[:, LAT:])
    tiles[rank] = jnp.concatenate(
        [fake_pred - real, jnp.abs(taken_latent - real)], axis=1
    )
    for k in range(1, ranks):
        send(tiles.at[rank], tiles.at[rank], 8, fellow(k))
    joined(tiles, 8, ranks - 1).wait_recv()
    all_tiles = tiles[...]
    gap = jnp.sum(all_tiles, axis=0)
    gap = gap[0:8] + gap[8:16]
    lane = lax.broadcasted_iota(jnp.int32, gap.shape, 1)
    gap = jnp.where(lane >= LAT, gap, 0.0)
    diff = all_tiles.reshape(tokens, 128)[:, :LAT]

    grad_rows = grad_ref.shape[0]
    start, skip = group * grad_rows, 0
    if grad_rows % 128:
        skip = (group % 2) * LAT
        start = start - skip
    found = lax.dot_general(
        act_student[:, pl.ds(pl.multiple_of(start, 128), window.shape[0])],
        jnp.concatenate(three_parts(diff), axis=1),
        (((0,), (0,)), ((), ())),
        preferred_element_type=F32,
    )
    window[...] = found[:, :LAT] + found[:, LAT : 2 * LAT] + found[:, 2 * LAT :]
    quarter = grad_rows // 8
    for column in range(COLUMNS):
        low_rows = pl.multiple_of(skip + column * quarter, 8)
        high_rows = pl.multiple_of(skip + grad_rows // 2 + column * quarter, 8)
        y_out[column, 0:quarter, :] = jnp.concatenate(
            [window[pl.ds(low_rows, quarter), :], window[pl.ds(high_rows, quarter), :]],
            axis=1,
        )
        y_out[column, quarter : quarter + 8, :] = gap
    for k in range(1, COLUMNS):
        other, target = in_row(k)
        send(y_out.at[other], y_in.at[y], 9, target)
    y_in[y] = y_out[y]
    joined(y_in, 9, COLUMNS - 1).wait_recv()
    sums = jnp.sum(y_in[...], axis=0)
    owners = quarter // 8
    for r in range(rows_z):
        z_out[r, 0:8, :] = (
            sums[8 * r : 8 * r + 8] if r < owners else jnp.zeros((8, 128), F32)
        )
        z_out[r, 8:16, :] = sums[quarter:]
    for k in range(1, rows_z):
        other, target = in_column(k)
        send(z_out.at[other], z_in.at[z], 10, target)
    z_in[z] = z_out[z]
    joined(z_in, 10, rows_z - 1).wait_recv()
    sums = jnp.sum(z_in[...], axis=0)
    gap_total = jnp.sum(sums[8:16, :], keepdims=True)
    scale = 1.0 / (gap_total / (tokens * seqs * LAT) + 1e-05)
    token_scale = float(tokens * seqs) ** -0.5

    @pl.when(z < owners)
    def _():
        pieces[z] = (scale * token_scale) * sums[0:8, :]
        for k in range(1, rows_z):
            _, target = in_column(k)
            send(pieces.at[z], pieces.at[z], 11, target)
        if owners > 1:
            joined(pieces, 11, owners - 1).wait_recv()

    if owners < rows_z:

        @pl.when(z >= owners)
        def _():
            joined(pieces, 11, owners).wait_recv()

    columns[y] = pieces[...].reshape(quarter, 128)
    for k in range(1, COLUMNS):
        _, target = in_row(k)
        send(columns.at[y], columns.at[y], 12, target)
    diff_ref[...] = scale * diff
    joined(columns, 12, COLUMNS - 1).wait_recv()
    complete = columns[...].reshape(grad_rows // 2, 128)
    grad_ref[0 : grad_rows // 2, :] = complete[:, :LAT]
    grad_ref[grad_rows // 2 :, :] = complete[:, LAT:]

    def left(src, dst, sem):
        copy_to(src, dst, one_send.at[sem], one_recv.at[sem], here).wait_send()

    left(key_hbm.at[:, other_columns], k_weights.at[mine, z], 0)
    left(query_hbm.at[:, other_columns], q_weights.at[mine, z], 13)
    left(value_hbm.at[:, other_columns], value_mail, 1)
    left(down_hbm, down_mail, 14)
    left(act.at[side, this_half], act.at[side, this_half], 5)
    left(act.at[1 - side, this_half], act.at[1 - side, this_half], 15)
    joined(fold_column, 2, COLUMNS - 1).wait_send()
    joined(fold_rows, 3, rows_z - 1).wait_send()
    joined(fold_whole, 4, rows_z - 1).wait_send()
    joined(share, 6, members - 1).wait_send()
    joined(halves, 7, 1).wait_send()
    joined(tiles, 8, ranks - 1).wait_send()
    joined(y_out, 9, COLUMNS - 1).wait_send()
    joined(z_out, 10, rows_z - 1).wait_send()

    @pl.when(z < owners)
    def _():
        for _ in range(1, rows_z):
            joined(pieces, 11, 1).wait_send()

    joined(columns, 12, COLUMNS - 1).wait_send()
    for chain in (kw, qw, vw, dw, ka, kb, vs):
        chain.drain()


def local(
    student_hidden_states,
    student_norm_gain,
    student_output_head,
    noise,
    timestep,
    context,
    patch_embedding_input,
    attention_norm_gain,
    query_weight,
    key_weight,
    value_weight,
    adapter_down_weight,
    adapter_up_weight,
    output_weight,
    velocity_head_output,
):
    tokens, width = student_hidden_states.shape
    depth = query_weight.shape[0]
    seqs = lax.axis_size("seq")
    rows_z = seqs // COLUMNS
    groups = lax.axis_size("grp") * lax.axis_size("tp")
    ranks = 2 * lax.axis_size("tp")
    grad_rows = width // groups
    window = grad_rows + LAT if grad_rows % 128 else grad_rows
    quarter = grad_rows // 8
    vmem = pl.BlockSpec(memory_space=pltpu.VMEM)
    smem = pl.BlockSpec(memory_space=pltpu.SMEM)
    dma = pltpu.SemaphoreType.DMA
    chain = [dma((3 * rows_z,)), dma((2 * rows_z,))]
    return pl.pallas_call(
        functools.partial(kernel, rows_z),
        out_shape=(
            jax.ShapeDtypeStruct((tokens, LAT), F32),
            jax.ShapeDtypeStruct((grad_rows, LAT), F32),
        ),
        in_specs=[smem] + [pl.BlockSpec(memory_space=pl.ANY)] * 14,
        out_specs=(vmem, vmem),
        scratch_shapes=[
            pltpu.VMEM((tokens, width), BF16),
            pltpu.VMEM((1, width), F32),
            pltpu.VMEM((LAT, width), BF16),
            pltpu.VMEM((LAT, tokens), BF16),
            pltpu.VMEM((tokens, width), BF16),
            pltpu.VMEM((LAT, width), BF16),
            pltpu.VMEM((1, width), F32),
            pltpu.VMEM(adapter_up_weight.shape, BF16),
            pltpu.VMEM((depth, 2 * HEAD_WIDTH), BF16),
            pltpu.VMEM((LAT, width), BF16),
            pltpu.VMEM((LAT, depth), BF16),
            pltpu.VMEM((LAT, depth), BF16),
            pltpu.VMEM((depth, HEAD_WIDTH), BF16),
            pltpu.VMEM((depth, HEAD_WIDTH), BF16),
            pltpu.VMEM((COLUMNS, rows_z, depth, HEAD_WIDTH), BF16),
            pltpu.VMEM((COLUMNS, rows_z, depth, HEAD_WIDTH), BF16),
            pltpu.VMEM((2, rows_z, depth, 2 * LAT), BF16),
            pltpu.VMEM((2, rows_z, depth, 2 * LAT), BF16),
            pltpu.VMEM((256 if depth % 128 else depth, 256), BF16),
            pltpu.VMEM((2, LAT, HEAD_WIDTH), F32),
            pltpu.VMEM((COLUMNS, LAT, HEAD_WIDTH), F32),
            pltpu.VMEM((rows_z, LAT // rows_z, HEAD_WIDTH), F32),
            pltpu.VMEM((rows_z, LAT // rows_z, HEAD_WIDTH), F32),
            pltpu.VMEM((rows_z, LAT // rows_z, HEAD_WIDTH), F32),
            pltpu.VMEM((tokens, width), BF16),
            pltpu.VMEM((tokens, width), F32),
            pltpu.VMEM((2, tokens, width), BF16),
            pltpu.VMEM((2, tokens, LAT), F32),
            pltpu.VMEM((2 * tokens, HEAD_WIDTH), F32),
            pltpu.VMEM((2 * tokens, HEAD_WIDTH), F32),
            pltpu.VMEM((2 * tokens, LAT), F32),
            pltpu.VMEM((2 * tokens, LAT), F32),
            pltpu.VMEM((2, rows_z, 2 * tokens, HEAD_WIDTH), BF16),
            pltpu.VMEM((2, rows_z, tokens, 128), BF16),
            pltpu.VMEM((2 * rows_z, 4 * tokens, 2 * tokens), F32),
            pltpu.VMEM((4 * tokens, tokens), F32),
            pltpu.VMEM((4 * tokens, tokens), F32),
            pltpu.VMEM((4 * tokens, LAT), F32),
            pltpu.VMEM((2 * ranks, 16, 128), F32),
            pltpu.VMEM((2 * ranks, 16, 128), F32),
            pltpu.VMEM((2, 16, 128), F32),
            pltpu.VMEM((ranks, 16, 128), F32),
            pltpu.VMEM((window, LAT), F32),
            pltpu.VMEM((COLUMNS, quarter + 8, 128), F32),
            pltpu.VMEM((COLUMNS, quarter + 8, 128), F32),
            pltpu.VMEM((rows_z, 16, 128), F32),
            pltpu.VMEM((rows_z, 16, 128), F32),
            pltpu.VMEM((quarter // 8, 8, 128), F32),
            pltpu.VMEM((COLUMNS, quarter, 128), F32),
        ]
        + chain * 7
        + [dma((16,)), dma((16,)), dma((14,))],
        compiler_params=pltpu.CompilerParams(
            collective_id=0, has_side_effects=True, vmem_limit_bytes=60 * MIB
        ),
    )(
        timestep,
        student_hidden_states,
        student_norm_gain.reshape(1, width),
        student_output_head.T,
        noise.T,
        context,
        patch_embedding_input,
        attention_norm_gain.reshape(1, width),
        query_weight,
        key_weight,
        value_weight,
        adapter_down_weight.T,
        adapter_up_weight,
        output_weight.T,
        velocity_head_output.T,
    )


def solution(mesh):
    heads = P("seq", ("grp", "tp"))
    in_specs = (
        P("seq", None),
        P(),
        P(),
        P("seq", None),
        P(),
        P("seq", None),
        P(),
        P(),
        heads,
        heads,
        heads,
        P("seq", None),
        P(None, ("grp", "tp")),
        P(("grp", "tp"), "seq"),
        P(),
    )
    out_specs = (P("seq", None), P(("grp", "tp"), None))
    return jax.shard_map(local, mesh=mesh, in_specs=in_specs, out_specs=out_specs, check_vma=False)
```

```python
import functools

import jax
import jax.numpy as jnp
from jax import lax
from jax.experimental import pallas as pl
from jax.experimental.pallas import tpu as pltpu
from jax.sharding import PartitionSpec as P

HEAD_WIDTH = 128
LAT = 64
COLUMNS = 4
EPS = 1e-06
F32 = jnp.float32
BF16 = jnp.bfloat16
MIB = 1024 * 1024


def position(rows_z):
    seq = lax.axis_index("seq")
    y, z = seq // rows_z, seq % rows_z
    side = y // 2
    pair = jnp.where(y < 2, y, 3 - y)
    partner = (3 - y) * rows_z + z
    sibling = (y + 1 - 2 * (y % 2)) * rows_z + z
    return seq, y, z, side, pair, partner, sibling


def copy_to(src, dst, send_sem, recv_sem, target):
    return pltpu.make_async_remote_copy(
        src_ref=src,
        dst_ref=dst,
        send_sem=send_sem,
        recv_sem=recv_sem,
        device_id=target,
        device_id_type=pl.DeviceIdType.MESH,
    )


class Chain:
    def __init__(self, unit, send_sem, recv_sem, rows_z, only=None):
        self.unit, self.send_sem, self.recv_sem, self.rows_z = unit, send_sem, recv_sem, rows_z
        self.only = only
        (self.seq, _, self.z, _, self.pair, _, self.sibling) = position(rows_z)

    def moves(self, row, condition):
        return condition if self.only is None else jnp.logical_and(condition, row == self.only)

    def copy(self, pair, row, way, target):
        ref = self.unit(pair, row)
        return copy_to(
            ref,
            ref,
            self.send_sem.at[way * self.rows_z + row],
            self.recv_sem.at[pair * self.rows_z + row],
            {"seq": target},
        )

    def up(self, row):
        return self.copy(self.pair, row, 0, jnp.minimum(self.seq + 1, 4 * self.rows_z - 1))

    def down(self, row):
        return self.copy(self.pair, row, 1, jnp.maximum(self.seq - 1, 0))

    def across(self, row):
        return self.copy(self.pair, row, 2, self.sibling)

    def own(self):
        z = self.z

        @pl.when(self.moves(z, z < self.rows_z - 1))
        def _():
            self.up(z).start()

        @pl.when(self.moves(z, z > 0))
        def _():
            self.down(z).start()

        if self.only is None:
            self.across(z).start()
        else:

            @pl.when(z == self.only)
            def _():
                self.across(z).start()

    def step(self, t):
        z, last = self.z, self.rows_z - 1

        @pl.when(self.moves(z - t, z - t >= 0))
        def _():
            row = z - t
            self.up(row).wait_recv()

            @pl.when(z < last)
            def _():
                self.up(row).start()

            self.across(row).start()

        @pl.when(self.moves(z + t, z + t <= last))
        def _():
            row = z + t
            self.down(row).wait_recv()

            @pl.when(z > 0)
            def _():
                self.down(row).start()

            self.across(row).start()

    def sibling_recv(self):
        def body(row, carry):
            @pl.when(self.moves(row, row >= 0))
            def _():
                self.copy(1 - self.pair, row, 2, self.sibling).wait_recv()

            return carry

        lax.fori_loop(0, self.rows_z, body, 0)

    def drain(self):
        z, last = self.z, self.rows_z - 1

        def body(row, carry):
            @pl.when(self.moves(row, jnp.logical_and(z < last, row <= z)))
            def _():
                self.up(row).wait_send()

            @pl.when(self.moves(row, jnp.logical_and(z > 0, row >= z)))
            def _():
                self.down(row).wait_send()

            @pl.when(self.moves(row, row >= 0))
            def _():
                self.across(row).wait_send()

            return carry

        lax.fori_loop(0, self.rows_z, body, 0)


def noise_level_of(timestep_ref):
    fraction = jnp.full((1, LAT), timestep_ref[0], jnp.int32).astype(F32) / 1000.0
    return 5.0 * fraction / (1.0 + 4.0 * fraction)


def three_parts(value):
    high = value.astype(BF16)
    rest = value - high.astype(F32)
    middle = rest.astype(BF16)
    low = (rest - middle.astype(F32)).astype(BF16)
    return high, middle, low


def kernel(
    rows_z,
    timestep_ref,
    student_hbm,
    student_gain_hbm,
    student_head_hbm,
    noise_hbm,
    context_hbm,
    patch_hbm,
    gain_hbm,
    query_hbm,
    key_hbm,
    value_hbm,
    down_hbm,
    up_hbm,
    output_hbm,
    velocity_hbm,
    diff_ref,
    grad_ref,
    student_ref,
    student_gain_ref,
    student_head_ref,
    noise_ref,
    context_ref,
    patch_ref,
    gain_ref,
    up_ref,
    output_ref,
    velocity_ref,
    down_own,
    down_mail,
    value_own,
    value_mail,
    k_weights,
    q_weights,
    v_weights,
    down_weights,
    down_placed,
    placed,
    fold_out,
    fold_column,
    fold_rows,
    fold_arrived,
    fold_whole,
    act_student,
    hidden,
    act,
    latents,
    k_product,
    q_product,
    v_product,
    low_out,
    low_in,
    low_tiles,
    keys,
    values,
    scores,
    top,
    total,
    mixed,
    share,
    met,
    halves,
    tiles,
    window,
    y_out,
    y_in,
    z_out,
    z_in,
    pieces,
    columns,
    kw_send,
    kw_recv,
    qw_send,
    qw_recv,
    vw_send,
    vw_recv,
    dw_send,
    dw_recv,
    ka_send,
    ka_recv,
    kb_send,
    kb_recv,
    v_send,
    v_recv,
    one_send,
    one_recv,
    load_sem,
):
    seq, y, z, side, pair, partner, sibling = position(rows_z)
    tokens, width = student_ref.shape
    depth = query_hbm.shape[0]
    tp_size = lax.axis_size("tp")
    tp = lax.axis_index("tp")
    grp = lax.axis_index("grp")
    groups = lax.axis_size("grp") * tp_size
    group = grp * tp_size + tp
    z_hi, core = grp // 2, grp % 2
    ranks = 2 * tp_size
    rank = core * tp_size + tp
    members = 2 * ranks
    me = side * ranks + rank
    span = width // COLUMNS
    seqs = COLUMNS * rows_z
    here = {"seq": partner}

    def member(k):
        j = (me + k) % members
        column = jnp.where(j // ranks == 0, pair, 3 - pair)
        r = j % ranks
        return j, {
            "grp": z_hi * 2 + r // tp_size,
            "seq": column * rows_z + z,
            "tp": r % tp_size,
        }

    def fellow(k):
        r = (rank + k) % ranks
        return {"grp": z_hi * 2 + r // tp_size, "tp": r % tp_size}

    def in_column(k):
        other = (z + k) % rows_z
        return other, {"seq": y * rows_z + other}

    def in_row(k):
        other = (y + k) % COLUMNS
        return other, {"seq": other * rows_z + z}

    def joined(ref, sem, count):
        part = ref.at[pl.ds(0, count)]
        return copy_to(part, part, one_send.at[sem], one_recv.at[sem], here)

    def send(src, dst, sem, target):
        copy_to(src, dst, one_send.at[sem], one_recv.at[sem], target).start()

    own_columns = pl.ds(pl.multiple_of(side * HEAD_WIDTH, HEAD_WIDTH), HEAD_WIDTH)
    other_columns = pl.ds(pl.multiple_of((1 - side) * HEAD_WIDTH, HEAD_WIDTH), HEAD_WIDTH)
    mine = 2 * pair + side
    theirs = 2 * pair + 1 - side
    sources = (
        (output_hbm, output_ref),
        (velocity_hbm, velocity_ref),
        (student_hbm, student_ref),
        (student_gain_hbm, student_gain_ref),
        (key_hbm.at[:, own_columns], k_weights.at[mine, z]),
        (query_hbm.at[:, own_columns], q_weights.at[mine, z]),
        (student_head_hbm, student_head_ref),
        (noise_hbm, noise_ref),
        (patch_hbm, patch_ref),
        (context_hbm, context_ref),
        (gain_hbm, gain_ref),
        (value_hbm.at[:, own_columns], value_own),
        (down_hbm, down_own),
        (up_hbm, up_ref),
    )
    loads = [
        pltpu.make_async_copy(src, dst, load_sem.at[i]) for i, (src, dst) in enumerate(sources)
    ]
    for load in loads:
        load.start()

    centre = rows_z // 2 - 1
    own_part = jnp.clip(z - centre, 0, 1)
    is_owner = jnp.logical_and(z >= centre, z <= centre + 1)

    def to_owners(parts, arrived, sem):
        for o in range(2):

            @pl.when(z != centre + o)
            def _():
                send(parts.at[o], arrived.at[z], sem, {"seq": y * rows_z + centre + o})

    def own_sum(parts, arrived, sem):
        arrived[z] = parts[own_part]
        joined(arrived, sem, rows_z - 1).wait_recv()
        return jnp.sum(arrived[...], axis=0)

    def from_owner(whole, sem):
        for k in range(1, rows_z):
            _, target = in_column(k)
            send(whole.at[own_part], whole.at[own_part], sem, target)

    def owners_done(whole, sem):
        @pl.when(is_owner)
        def _():
            joined(whole, sem, 1).wait_recv()

        @pl.when(jnp.logical_not(is_owner))
        def _():
            joined(whole, sem, 2).wait_recv()

    def owners_left(parts, arrived, whole, first_sem, second_sem):
        @pl.when(is_owner)
        def _():
            joined(parts, first_sem, 1).wait_send()
            joined(arrived, second_sem, rows_z - 1).wait_send()

        @pl.when(jnp.logical_not(is_owner))
        def _():
            joined(parts, first_sem, 2).wait_send()

    barrier = pltpu.get_barrier_semaphore()

    def greet(target):
        pl.semaphore_signal(
            barrier, inc=1, device_id=target, device_id_type=pl.DeviceIdType.MESH
        )

    for k in range(1, COLUMNS):
        greet(in_row(k)[1])
    for k in range(1, rows_z):
        greet(in_column(k)[1])
    for k in range(1, members):
        if k != ranks:
            greet(member(k)[1])
    greet({"grp": (1 - z_hi) * 2 + core})

    loads[0].wait()
    loads[1].wait()
    wide = placed.shape[0]
    begin = seq * depth
    offset = begin % 128
    placed[...] = jnp.zeros(placed.shape, BF16)
    placed[pl.ds(pl.multiple_of(offset, 32), depth), :] = output_ref[...]
    folded = jnp.dot(
        velocity_ref[:, pl.ds(pl.multiple_of(begin - offset, 128), wide)],
        placed[...],
        preferred_element_type=F32,
    )
    fold_out[0] = folded[:, :HEAD_WIDTH]
    fold_out[1] = folded[:, HEAD_WIDTH:]
    fold_column[y] = fold_out[side]

    pl.semaphore_wait(barrier, 1 + COLUMNS - 1 + rows_z - 1 + members - 2)

    send(key_hbm.at[:, other_columns], k_weights.at[mine, z], 0, here)
    for k in range(1, COLUMNS):
        other, target = in_row(k)
        send(fold_out.at[other // 2], fold_column.at[y], 2, target)
    send(query_hbm.at[:, other_columns], q_weights.at[mine, z], 13, here)
    send(value_hbm.at[:, other_columns], value_mail, 1, here)
    send(down_hbm, down_mail, 14, here)
    loads[2].wait()
    loads[3].wait()

    chunk = 16

    def student_rows(i, carry):
        rows = pl.ds(pl.multiple_of(i * chunk, chunk), chunk)
        value = student_ref[rows, :].astype(F32)
        scale = lax.rsqrt(jnp.mean(value * value, axis=-1, keepdims=True) + EPS)
        act_student[rows, :] = (value * scale * student_gain_ref[...]).astype(BF16)
        return carry

    lax.fori_loop(0, tokens // chunk, student_rows, 0)

    def came(src, dst, sem):
        copy_to(src, dst, one_send.at[sem], one_recv.at[sem], here).wait_recv()

    def two_slots(ref):
        return lambda p, r: ref.at[pl.ds(2 * p, 2), r]

    kw = Chain(two_slots(k_weights), kw_send, kw_recv, rows_z)
    qw = Chain(two_slots(q_weights), qw_send, qw_recv, rows_z)
    vw = Chain(lambda p, r: v_weights.at[p, r], vw_send, vw_recv, rows_z)
    dw = Chain(lambda p, r: down_weights.at[p], dw_send, dw_recv, rows_z, rank)
    loads[4].wait()
    came(key_hbm.at[:, other_columns], k_weights.at[theirs, z], 0)
    kw.own()

    joined(fold_column, 2, COLUMNS - 1).wait_recv()
    fold_rows[...] = jnp.sum(fold_column[...], axis=0).reshape(fold_rows.shape)
    to_owners(fold_rows, fold_arrived, 3)
    loads[5].wait()
    came(query_hbm.at[:, other_columns], q_weights.at[theirs, z], 13)
    qw.own()

    def in_order(own, other):
        lower = jnp.where(side == 0, own, other)
        upper = jnp.where(side == 0, other, own)
        return jnp.concatenate([lower, upper], axis=1).astype(BF16)

    loads[12].wait()
    came(down_hbm, down_mail, 14)

    @pl.when(z == rank)
    def _():
        down_weights[pair] = in_order(
            down_own[...].astype(F32).T, down_mail[...].astype(F32).T
        )

    dw.own()
    loads[6].wait()
    loads[7].wait()

    level = noise_level_of(timestep_ref)
    latent = lax.dot_general(
        act_student[...],
        student_head_ref[...],
        (((1,), (1,)), ((), ())),
        preferred_element_type=F32,
    )
    noise = noise_ref[...].astype(F32).T
    noisy = ((1.0 - level) * latent + level * noise).astype(BF16)
    loads[8].wait()
    loads[9].wait()
    slab = 512 if width % 512 == 0 else width

    def hidden_columns(i, carry):
        part = pl.ds(pl.multiple_of(i * slab, slab), slab)
        hidden[:, part] = jnp.dot(
            noisy, patch_ref[:, part], preferred_element_type=F32
        ) + context_ref[:, part].astype(F32)
        return carry

    lax.fori_loop(0, width // slab, hidden_columns, 0)

    kw.step(1)
    @pl.when(is_owner)
    def _():
        fold_whole[own_part] = own_sum(fold_rows, fold_arrived, 3)
        from_owner(fold_whole, 4)

    loads[10].wait()

    def act_rows(i, carry):
        rows = pl.ds(pl.multiple_of(i * chunk, chunk), chunk)
        value = hidden[rows, :]
        scale = lax.rsqrt(jnp.mean(value * value, axis=-1, keepdims=True) + EPS)
        act[side, rows, :] = (value * scale * gain_ref[...]).astype(BF16)
        return carry

    lax.fori_loop(0, tokens // chunk, act_rows, 0)
    half = tokens // 2
    this_half = pl.ds(pl.multiple_of(core * half, half), half)
    that_half = pl.ds(pl.multiple_of((1 - core) * half, half), half)
    send(act.at[side, this_half], act.at[side, this_half], 5, here)
    qw.step(1)
    kw.step(2)

    owners_done(fold_whole, 4)
    whole = fold_whole[...].reshape(LAT, HEAD_WIDTH)
    high = whole.astype(BF16)
    rest = (whole - high.astype(F32)).astype(BF16)
    split = jnp.concatenate([high, rest], axis=0)
    loads[11].wait()
    came(value_hbm.at[:, other_columns], value_mail, 1)

    def fold_value(ref):
        moved = lax.dot_general(
            ref[...], split, (((1,), (1,)), ((), ())), preferred_element_type=F32
        )
        return moved[:, :LAT] + moved[:, LAT:]

    v_weights[pair, z] = in_order(fold_value(value_own), fold_value(value_mail))
    vw.own()
    qw.step(2)

    taken = pl.ds(pl.multiple_of(rank * 16, 16), 16)
    latents[0] = latent
    latents[1] = noisy.astype(F32)
    parts = jnp.concatenate(three_parts(hidden[taken, :]), axis=0)
    residual = lax.dot_general(
        parts, velocity_ref[...], (((1,), (1,)), ((), ())), preferred_element_type=F32
    )
    residual = residual[0:16] + residual[16:32] + residual[32:48]

    def weight_steps(t, carry):
        kw.step(t + 2)
        vw.step(t)
        qw.step(t + 2)
        dw.step(t)
        return carry

    middle = min(4, rows_z)
    lax.fori_loop(1, middle, weight_steps, 0)
    came(act.at[1 - side, this_half], act.at[1 - side, this_half], 5)
    core_mate = {"grp": grp + 1 - 2 * core}
    send(act.at[1 - side, this_half], act.at[1 - side, this_half], 15, core_mate)
    lax.fori_loop(middle, rows_z, weight_steps, 0)
    came(act.at[1 - side, that_half], act.at[1 - side, that_half], 15)

    def rows_at(column):
        part = pl.ds(pl.multiple_of(column * span, span), span)
        return act[:, :, part].reshape(2 * tokens, span)

    def project(weights, p):
        lower = jnp.dot(
            rows_at(p), weights[2 * p].reshape(span, 128), preferred_element_type=F32
        )
        upper = jnp.dot(
            rows_at(3 - p), weights[2 * p + 1].reshape(span, 128), preferred_element_type=F32
        )
        return lower + upper

    def project_packed(weights, p):
        packed = weights[p].reshape(span, 128)
        lower = jnp.dot(rows_at(p), packed, preferred_element_type=F32)
        upper = jnp.dot(rows_at(3 - p), packed, preferred_element_type=F32)
        return lower[:, :LAT] + upper[:, LAT:]

    dw.sibling_recv()
    row = jnp.minimum(rank, rows_z - 1)
    shift = (row * depth) % 128
    down_placed[...] = jnp.zeros(down_placed.shape, BF16)
    for p in range(2):
        down_placed[p, pl.ds(pl.multiple_of(shift, 32), depth), :] = down_weights[p]

    def low_term(column, p):
        part = pl.ds(pl.multiple_of(column * span + row * depth - shift, 128), wide)
        rows = act[:, :, part].reshape(2 * tokens, wide)
        return jnp.dot(rows, down_placed[p], preferred_element_type=F32)

    low_sum = (
        low_term(0, 0)[:, :LAT]
        + low_term(3, 0)[:, LAT:]
        + low_term(1, 1)[:, :LAT]
        + low_term(2, 1)[:, LAT:]
    )
    low_sum = jnp.where(rank < rows_z, low_sum, 0.0)
    low_out[...] = jnp.concatenate([low_sum[:tokens], low_sum[tokens:]], axis=1).reshape(
        low_out.shape
    )
    for k in range(1, ranks):
        send(low_out.at[(rank + k) % ranks], low_in.at[rank], 16, fellow(k))
    low_in[rank] = low_out[rank]
    k_product[...] = project(k_weights, pair)
    kw.sibling_recv()
    keys[pair, z] = (k_product[...] + project(k_weights, 1 - pair)).astype(BF16)
    ka = Chain(lambda p, r: keys.at[p, r, pl.ds(0, tokens)], ka_send, ka_recv, rows_z)
    kb = Chain(lambda p, r: keys.at[p, r, pl.ds(tokens, tokens)], kb_send, kb_recv, rows_z)
    vs = Chain(lambda p, r: values.at[p, r], v_send, v_recv, rows_z)
    ka.own()
    kb.own()
    joined(low_in, 16, ranks - 1).wait_recv()
    low_tiles[rank] = jnp.sum(low_in[...], axis=0).astype(BF16)
    for k in range(1, ranks):
        send(low_tiles.at[rank], low_tiles.at[rank], 17, fellow(k))
    v_product[...] = project_packed(v_weights, pair)
    vw.sibling_recv()
    moved = (v_product[...] + project_packed(v_weights, 1 - pair)).astype(BF16)
    values[pair, z] = jnp.concatenate([moved[:tokens], moved[tokens:]], axis=1)
    vs.own()
    q_product[...] = project(q_weights, pair)
    qw.sibling_recv()
    plain = q_product[...] + project(q_weights, 1 - pair)
    joined(low_tiles, 17, ranks - 1).wait_recv()
    low = low_tiles[...].reshape(tokens, 2 * LAT)
    low = jnp.concatenate([low[:, :LAT], low[:, LAT:]], axis=0)
    loads[13].wait()
    fake = plain + jnp.dot(low, up_ref[:, own_columns], preferred_element_type=F32)
    asked = jnp.concatenate([plain, fake], axis=0).astype(BF16)
    top[...] = jnp.full(top.shape, -1e30, F32)
    factor = HEAD_WIDTH**-0.5

    def score_unit(p, r):
        found = (
            lax.dot_general(
                asked, keys[p, r], (((1,), (1,)), ((), ())), preferred_element_type=F32
            )
            * factor
        )
        scores[p * rows_z + r] = found
        top[...] = jnp.maximum(
            top[...], jnp.maximum(found[:, :tokens], found[:, tokens:])
        )

    def kv_steps(t, carry):
        ka.step(t)
        kb.step(t)
        vs.step(t)

        def way(d, carry):
            r = z + (1 - 2 * d) * (t - 1)
            fits = jnp.logical_and(r >= 0, r < rows_z)

            @pl.when(jnp.logical_and(fits, jnp.logical_or(t > 1, d == 0)))
            def _():
                score_unit(pair, r)

            return carry

        lax.fori_loop(0, 2, way, 0)
        return carry

    lax.fori_loop(1, rows_z + 1, kv_steps, 0)

    def from_sibling(r, carry):
        ka.copy(1 - pair, r, 2, sibling).wait_recv()
        kb.copy(1 - pair, r, 2, sibling).wait_recv()
        score_unit(1 - pair, r)
        return carry

    lax.fori_loop(0, rows_z, from_sibling, 0)
    vs.sibling_recv()
    peak = jnp.max(top[...], axis=-1, keepdims=True)
    top[...] = jnp.broadcast_to(peak, top.shape)
    total[...] = jnp.zeros(total.shape, F32)
    mixed[...] = jnp.zeros(mixed.shape, F32)

    def mix_unit(u, carry):
        shift = top[...]
        left = jnp.exp(scores[u, :, 0:tokens] - shift)
        right = jnp.exp(scores[u, :, tokens : 2 * tokens] - shift)
        total[...] += left + right
        packed = values[u // rows_z, u % rows_z]
        stacked = jnp.concatenate([packed[:, :LAT], packed[:, LAT:]], axis=0)
        mixed[...] += jnp.dot(
            jnp.concatenate([left, right], axis=1).astype(BF16),
            stacked,
            preferred_element_type=F32,
        )
        return carry

    lax.fori_loop(0, 2 * rows_z, mix_unit, 0)
    attended = mixed[...] / jnp.sum(total[...], axis=-1, keepdims=True)
    share[...] = jnp.concatenate(
        [attended[: 2 * tokens], attended[2 * tokens :]], axis=1
    ).reshape(share.shape)

    for k in range(1, members):
        j, target = member(k)
        send(share.at[j], met.at[me], 6, target)
    met[me] = share[me]
    joined(met, 6, members - 1).wait_recv()
    halves[0] = jnp.sum(met[...], axis=0)
    send(halves.at[0], halves.at[1], 7, {"grp": (1 - z_hi) * 2 + core})
    joined(halves, 7, 1).wait_recv()
    shares = halves[0] + halves[1]
    taken_latent = latents[0, taken, :]
    taken_noisy = latents[1, taken, :]
    real = taken_noisy - level * (residual + shares[:, :LAT])
    fake_pred = taken_noisy - level * (residual + shares[:, LAT:])
    tiles[rank] = jnp.concatenate(
        [fake_pred - real, jnp.abs(taken_latent - real)], axis=1
    )
    for k in range(1, ranks):
        send(tiles.at[rank], tiles.at[rank], 8, fellow(k))
    joined(tiles, 8, ranks - 1).wait_recv()
    all_tiles = tiles[...]
    gap = jnp.sum(all_tiles, axis=0)
    gap = gap[0:8] + gap[8:16]
    lane = lax.broadcasted_iota(jnp.int32, gap.shape, 1)
    gap = jnp.where(lane >= LAT, gap, 0.0)
    diff = all_tiles.reshape(tokens, 128)[:, :LAT]

    grad_rows = grad_ref.shape[0]
    start, skip = group * grad_rows, 0
    if grad_rows % 128:
        skip = (group % 2) * LAT
        start = start - skip
    found = lax.dot_general(
        act_student[:, pl.ds(pl.multiple_of(start, 128), window.shape[0])],
        jnp.concatenate(three_parts(diff), axis=1),
        (((0,), (0,)), ((), ())),
        preferred_element_type=F32,
    )
    window[...] = found[:, :LAT] + found[:, LAT : 2 * LAT] + found[:, 2 * LAT :]
    quarter = grad_rows // 8
    for column in range(COLUMNS):
        low_rows = pl.multiple_of(skip + column * quarter, 8)
        high_rows = pl.multiple_of(skip + grad_rows // 2 + column * quarter, 8)
        y_out[column, 0:quarter, :] = jnp.concatenate(
            [window[pl.ds(low_rows, quarter), :], window[pl.ds(high_rows, quarter), :]],
            axis=1,
        )
        y_out[column, quarter : quarter + 8, :] = gap
    for k in range(1, COLUMNS):
        other, target = in_row(k)
        send(y_out.at[other], y_in.at[y], 9, target)
    y_in[y] = y_out[y]
    joined(y_in, 9, COLUMNS - 1).wait_recv()
    sums = jnp.sum(y_in[...], axis=0)
    share_rows = z_out.shape[1] - 8
    z_out[0, 0:share_rows, :] = sums[0:share_rows]
    z_out[1, 0 : quarter - share_rows, :] = sums[share_rows:quarter]
    if quarter < 2 * share_rows:
        z_out[1, quarter - share_rows : share_rows, :] = jnp.zeros(
            (2 * share_rows - quarter, 128), F32
        )
    for o in range(2):
        z_out[o, share_rows : share_rows + 8, :] = sums[quarter:]
    to_owners(z_out, z_in, 10)
    token_scale = float(tokens * seqs) ** -0.5

    @pl.when(is_owner)
    def _():
        summed = own_sum(z_out, z_in, 10)
        gap_total = jnp.sum(summed[share_rows:], keepdims=True)
        factor = 1.0 / (gap_total / (tokens * seqs * LAT) + 1e-05)
        pieces[own_part, 0:share_rows, :] = (factor * token_scale) * summed[0:share_rows]
        pieces[own_part, share_rows : share_rows + 8, :] = jnp.broadcast_to(factor, (8, 128))
        from_owner(pieces, 11)

    owners_done(pieces, 11)
    scale = pieces[0, share_rows : share_rows + 1, 0:1]
    columns[y, 0:share_rows, :] = pieces[0, 0:share_rows, :]
    columns[y, share_rows:quarter, :] = pieces[1, 0 : quarter - share_rows, :]
    for k in range(1, COLUMNS):
        _, target = in_row(k)
        send(columns.at[y], columns.at[y], 12, target)
    diff_ref[...] = scale * diff
    joined(columns, 12, COLUMNS - 1).wait_recv()
    complete = columns[...].reshape(grad_rows // 2, 128)
    grad_ref[0 : grad_rows // 2, :] = complete[:, :LAT]
    grad_ref[grad_rows // 2 :, :] = complete[:, LAT:]

    def left(src, dst, sem):
        copy_to(src, dst, one_send.at[sem], one_recv.at[sem], here).wait_send()

    left(key_hbm.at[:, other_columns], k_weights.at[mine, z], 0)
    left(query_hbm.at[:, other_columns], q_weights.at[mine, z], 13)
    left(value_hbm.at[:, other_columns], value_mail, 1)
    left(down_hbm, down_mail, 14)
    joined(low_out, 16, ranks - 1).wait_send()
    joined(low_tiles, 17, ranks - 1).wait_send()
    left(act.at[side, this_half], act.at[side, this_half], 5)
    left(act.at[1 - side, this_half], act.at[1 - side, this_half], 15)
    joined(fold_column, 2, COLUMNS - 1).wait_send()
    owners_left(fold_rows, fold_arrived, fold_whole, 3, 4)
    joined(share, 6, members - 1).wait_send()
    joined(halves, 7, 1).wait_send()
    joined(tiles, 8, ranks - 1).wait_send()
    joined(y_out, 9, COLUMNS - 1).wait_send()
    owners_left(z_out, z_in, pieces, 10, 11)
    joined(columns, 12, COLUMNS - 1).wait_send()
    for chain in (kw, qw, vw, dw, ka, kb, vs):
        chain.drain()


def local(
    student_hidden_states,
    student_norm_gain,
    student_output_head,
    noise,
    timestep,
    context,
    patch_embedding_input,
    attention_norm_gain,
    query_weight,
    key_weight,
    value_weight,
    adapter_down_weight,
    adapter_up_weight,
    output_weight,
    velocity_head_output,
):
    tokens, width = student_hidden_states.shape
    depth = query_weight.shape[0]
    seqs = lax.axis_size("seq")
    rows_z = seqs // COLUMNS
    groups = lax.axis_size("grp") * lax.axis_size("tp")
    ranks = 2 * lax.axis_size("tp")
    grad_rows = width // groups
    window = grad_rows + LAT if grad_rows % 128 else grad_rows
    quarter = grad_rows // 8
    share_rows = (quarter // 8 + 1) // 2 * 8
    wide = 256 if depth % 128 else depth
    vmem = pl.BlockSpec(memory_space=pltpu.VMEM)
    smem = pl.BlockSpec(memory_space=pltpu.SMEM)
    dma = pltpu.SemaphoreType.DMA
    chain = [dma((3 * rows_z,)), dma((2 * rows_z,))]
    return pl.pallas_call(
        functools.partial(kernel, rows_z),
        out_shape=(
            jax.ShapeDtypeStruct((tokens, LAT), F32),
            jax.ShapeDtypeStruct((grad_rows, LAT), F32),
        ),
        in_specs=[smem] + [pl.BlockSpec(memory_space=pl.ANY)] * 14,
        out_specs=(vmem, vmem),
        scratch_shapes=[
            pltpu.VMEM((tokens, width), BF16),
            pltpu.VMEM((1, width), F32),
            pltpu.VMEM((LAT, width), BF16),
            pltpu.VMEM((LAT, tokens), BF16),
            pltpu.VMEM((tokens, width), BF16),
            pltpu.VMEM((LAT, width), BF16),
            pltpu.VMEM((1, width), F32),
            pltpu.VMEM(adapter_up_weight.shape, BF16),
            pltpu.VMEM((depth, 2 * HEAD_WIDTH), BF16),
            pltpu.VMEM((LAT, width), BF16),
            pltpu.VMEM((LAT, depth), BF16),
            pltpu.VMEM((LAT, depth), BF16),
            pltpu.VMEM((depth, HEAD_WIDTH), BF16),
            pltpu.VMEM((depth, HEAD_WIDTH), BF16),
            pltpu.VMEM((COLUMNS, rows_z, depth, HEAD_WIDTH), BF16),
            pltpu.VMEM((COLUMNS, rows_z, depth, HEAD_WIDTH), BF16),
            pltpu.VMEM((2, rows_z, depth, 2 * LAT), BF16),
            pltpu.VMEM((2, depth, 2 * LAT), BF16),
            pltpu.VMEM((2, wide, 2 * LAT), BF16),
            pltpu.VMEM((wide, 256), BF16),
            pltpu.VMEM((2, LAT, HEAD_WIDTH), F32),
            pltpu.VMEM((COLUMNS, LAT, HEAD_WIDTH), F32),
            pltpu.VMEM((2, LAT // 2, HEAD_WIDTH), F32),
            pltpu.VMEM((rows_z, LAT // 2, HEAD_WIDTH), F32),
            pltpu.VMEM((2, LAT // 2, HEAD_WIDTH), F32),
            pltpu.VMEM((tokens, width), BF16),
            pltpu.VMEM((tokens, width), F32),
            pltpu.VMEM((2, tokens, width), BF16),
            pltpu.VMEM((2, tokens, LAT), F32),
            pltpu.VMEM((2 * tokens, HEAD_WIDTH), F32),
            pltpu.VMEM((2 * tokens, HEAD_WIDTH), F32),
            pltpu.VMEM((2 * tokens, LAT), F32),
            pltpu.VMEM((ranks, tokens // ranks, 2 * LAT), F32),
            pltpu.VMEM((ranks, tokens // ranks, 2 * LAT), F32),
            pltpu.VMEM((ranks, tokens // ranks, 2 * LAT), BF16),
            pltpu.VMEM((2, rows_z, 2 * tokens, HEAD_WIDTH), BF16),
            pltpu.VMEM((2, rows_z, tokens, 128), BF16),
            pltpu.VMEM((2 * rows_z, 4 * tokens, 2 * tokens), F32),
            pltpu.VMEM((4 * tokens, tokens), F32),
            pltpu.VMEM((4 * tokens, tokens), F32),
            pltpu.VMEM((4 * tokens, LAT), F32),
            pltpu.VMEM((2 * ranks, 16, 128), F32),
            pltpu.VMEM((2 * ranks, 16, 128), F32),
            pltpu.VMEM((2, 16, 128), F32),
            pltpu.VMEM((ranks, 16, 128), F32),
            pltpu.VMEM((window, LAT), F32),
            pltpu.VMEM((COLUMNS, quarter + 8, 128), F32),
            pltpu.VMEM((COLUMNS, quarter + 8, 128), F32),
            pltpu.VMEM((2, share_rows + 8, 128), F32),
            pltpu.VMEM((rows_z, share_rows + 8, 128), F32),
            pltpu.VMEM((2, share_rows + 8, 128), F32),
            pltpu.VMEM((COLUMNS, quarter, 128), F32),
        ]
        + chain * 7
        + [dma((18,)), dma((18,)), dma((14,))],
        compiler_params=pltpu.CompilerParams(
            collective_id=0, has_side_effects=True, vmem_limit_bytes=60 * MIB
        ),
    )(
        timestep,
        student_hidden_states,
        student_norm_gain.reshape(1, width),
        student_output_head.T,
        noise.T,
        context,
        patch_embedding_input,
        attention_norm_gain.reshape(1, width),
        query_weight,
        key_weight,
        value_weight,
        adapter_down_weight.T,
        adapter_up_weight,
        output_weight.T,
        velocity_head_output.T,
    )


def solution(mesh):
    heads = P("seq", ("grp", "tp"))
    in_specs = (
        P("seq", None),
        P(),
        P(),
        P("seq", None),
        P(),
        P("seq", None),
        P(),
        P(),
        heads,
        heads,
        heads,
        P("seq", None),
        P(None, ("grp", "tp")),
        P(("grp", "tp"), "seq"),
        P(),
    )
    out_specs = (P("seq", None), P(("grp", "tp"), None))
    return jax.shard_map(local, mesh=mesh, in_specs=in_specs, out_specs=out_specs, check_vma=False)
```

```python
import functools

import jax
import jax.numpy as jnp
from jax import lax
from jax.experimental import pallas as pl
from jax.experimental.pallas import tpu as pltpu
from jax.sharding import PartitionSpec as P

HEAD_WIDTH = 128
LAT = 64
COLUMNS = 4
EPS = 1e-06
F32 = jnp.float32
BF16 = jnp.bfloat16
MIB = 1024 * 1024


def position(rows_z):
    seq = lax.axis_index("seq")
    y, z = seq // rows_z, seq % rows_z
    side = y // 2
    pair = jnp.where(y < 2, y, 3 - y)
    partner = (3 - y) * rows_z + z
    sibling = (y + 1 - 2 * (y % 2)) * rows_z + z
    return seq, y, z, side, pair, partner, sibling


def copy_to(src, dst, send_sem, recv_sem, target):
    return pltpu.make_async_remote_copy(
        src_ref=src,
        dst_ref=dst,
        send_sem=send_sem,
        recv_sem=recv_sem,
        device_id=target,
        device_id_type=pl.DeviceIdType.MESH,
    )


class Chain:
    def __init__(self, unit, send_sem, recv_sem, rows_z, only=None):
        self.unit, self.send_sem, self.recv_sem, self.rows_z = unit, send_sem, recv_sem, rows_z
        self.only = only
        (self.seq, _, self.z, _, self.pair, _, self.sibling) = position(rows_z)

    def moves(self, row, condition):
        return condition if self.only is None else jnp.logical_and(condition, row == self.only)

    def copy(self, pair, row, way, target):
        ref = self.unit(pair, row)
        return copy_to(
            ref,
            ref,
            self.send_sem.at[way * self.rows_z + row],
            self.recv_sem.at[pair * self.rows_z + row],
            {"seq": target},
        )

    def up(self, row):
        return self.copy(self.pair, row, 0, jnp.minimum(self.seq + 1, 4 * self.rows_z - 1))

    def down(self, row):
        return self.copy(self.pair, row, 1, jnp.maximum(self.seq - 1, 0))

    def across(self, row):
        return self.copy(self.pair, row, 2, self.sibling)

    def own(self):
        z = self.z

        @pl.when(self.moves(z, z < self.rows_z - 1))
        def _():
            self.up(z).start()

        @pl.when(self.moves(z, z > 0))
        def _():
            self.down(z).start()

        if self.only is None:
            self.across(z).start()
        else:

            @pl.when(z == self.only)
            def _():
                self.across(z).start()

    def step(self, t):
        z, last = self.z, self.rows_z - 1

        @pl.when(self.moves(z - t, z - t >= 0))
        def _():
            row = z - t
            self.up(row).wait_recv()

            @pl.when(z < last)
            def _():
                self.up(row).start()

            self.across(row).start()

        @pl.when(self.moves(z + t, z + t <= last))
        def _():
            row = z + t
            self.down(row).wait_recv()

            @pl.when(z > 0)
            def _():
                self.down(row).start()

            self.across(row).start()

    def sibling_recv(self):
        def body(row, carry):
            @pl.when(self.moves(row, row >= 0))
            def _():
                self.copy(1 - self.pair, row, 2, self.sibling).wait_recv()

            return carry

        lax.fori_loop(0, self.rows_z, body, 0)

    def drain(self):
        z, last = self.z, self.rows_z - 1

        def body(row, carry):
            @pl.when(self.moves(row, jnp.logical_and(z < last, row <= z)))
            def _():
                self.up(row).wait_send()

            @pl.when(self.moves(row, jnp.logical_and(z > 0, row >= z)))
            def _():
                self.down(row).wait_send()

            @pl.when(self.moves(row, row >= 0))
            def _():
                self.across(row).wait_send()

            return carry

        lax.fori_loop(0, self.rows_z, body, 0)


def noise_level_of(timestep_ref):
    fraction = jnp.full((1, LAT), timestep_ref[0], jnp.int32).astype(F32) / 1000.0
    return 5.0 * fraction / (1.0 + 4.0 * fraction)


def three_parts(value):
    high = value.astype(BF16)
    rest = value - high.astype(F32)
    middle = rest.astype(BF16)
    low = (rest - middle.astype(F32)).astype(BF16)
    return high, middle, low


def kernel(
    rows_z,
    timestep_ref,
    student_hbm,
    student_gain_hbm,
    student_head_hbm,
    noise_hbm,
    context_hbm,
    patch_hbm,
    gain_hbm,
    query_hbm,
    key_hbm,
    value_hbm,
    down_hbm,
    up_hbm,
    output_hbm,
    velocity_hbm,
    diff_ref,
    grad_ref,
    student_ref,
    student_gain_ref,
    student_head_ref,
    noise_ref,
    context_ref,
    patch_ref,
    gain_ref,
    up_ref,
    output_ref,
    velocity_ref,
    down_own,
    down_mail,
    value_own,
    value_mail,
    k_weights,
    q_weights,
    v_weights,
    down_weights,
    down_placed,
    placed,
    fold_out,
    fold_column,
    fold_rows,
    fold_arrived,
    fold_whole,
    act_student,
    hidden,
    act,
    latents,
    k_product,
    q_product,
    v_product,
    low_out,
    low_in,
    low_tiles,
    keys,
    values,
    scores,
    top,
    total,
    mixed,
    share,
    met,
    halves,
    tiles,
    window,
    y_out,
    y_in,
    z_out,
    z_in,
    pieces,
    columns,
    kw_send,
    kw_recv,
    qw_send,
    qw_recv,
    vw_send,
    vw_recv,
    dw_send,
    dw_recv,
    ka_send,
    ka_recv,
    kb_send,
    kb_recv,
    v_send,
    v_recv,
    one_send,
    one_recv,
    load_sem,
):
    seq, y, z, side, pair, partner, sibling = position(rows_z)
    tokens, width = student_ref.shape
    depth = query_hbm.shape[0]
    tp_size = lax.axis_size("tp")
    tp = lax.axis_index("tp")
    grp = lax.axis_index("grp")
    groups = lax.axis_size("grp") * tp_size
    group = grp * tp_size + tp
    z_hi, core = grp // 2, grp % 2
    ranks = 2 * tp_size
    rank = core * tp_size + tp
    members = 2 * ranks
    me = side * ranks + rank
    span = width // COLUMNS
    seqs = COLUMNS * rows_z
    here = {"seq": partner}

    def member(k):
        j = (me + k) % members
        column = jnp.where(j // ranks == 0, pair, 3 - pair)
        r = j % ranks
        return j, {
            "grp": z_hi * 2 + r // tp_size,
            "seq": column * rows_z + z,
            "tp": r % tp_size,
        }

    def fellow(k):
        r = (rank + k) % ranks
        return {"grp": z_hi * 2 + r // tp_size, "tp": r % tp_size}

    def in_column(k):
        other = (z + k) % rows_z
        return other, {"seq": y * rows_z + other}

    def in_row(k):
        other = (y + k) % COLUMNS
        return other, {"seq": other * rows_z + z}

    def joined(ref, sem, count):
        part = ref.at[pl.ds(0, count)]
        return copy_to(part, part, one_send.at[sem], one_recv.at[sem], here)

    def send(src, dst, sem, target):
        copy_to(src, dst, one_send.at[sem], one_recv.at[sem], target).start()

    own_columns = pl.ds(pl.multiple_of(side * HEAD_WIDTH, HEAD_WIDTH), HEAD_WIDTH)
    other_columns = pl.ds(pl.multiple_of((1 - side) * HEAD_WIDTH, HEAD_WIDTH), HEAD_WIDTH)
    mine = 2 * pair + side
    theirs = 2 * pair + 1 - side
    sources = (
        (output_hbm, output_ref),
        (velocity_hbm, velocity_ref),
        (student_hbm, student_ref),
        (student_gain_hbm, student_gain_ref),
        (key_hbm.at[:, own_columns], k_weights.at[mine, z]),
        (query_hbm.at[:, own_columns], q_weights.at[mine, z]),
        (student_head_hbm, student_head_ref),
        (noise_hbm, noise_ref),
        (patch_hbm, patch_ref),
        (context_hbm, context_ref),
        (gain_hbm, gain_ref),
        (value_hbm.at[:, own_columns], value_own),
        (down_hbm, down_own),
        (up_hbm, up_ref),
    )
    loads = [
        pltpu.make_async_copy(src, dst, load_sem.at[i]) for i, (src, dst) in enumerate(sources)
    ]
    for load in loads:
        load.start()

    centre = rows_z // 2 - 1
    own_part = jnp.clip(z - centre, 0, 1)
    is_owner = jnp.logical_and(z >= centre, z <= centre + 1)

    def to_owners(parts, arrived, sem):
        for o in range(2):

            @pl.when(z != centre + o)
            def _():
                send(parts.at[o], arrived.at[z], sem, {"seq": y * rows_z + centre + o})

    def own_sum(parts, arrived, sem):
        arrived[z] = parts[own_part]
        joined(arrived, sem, rows_z - 1).wait_recv()
        return jnp.sum(arrived[...], axis=0)

    def from_owner(whole, sem):
        for k in range(1, rows_z):
            _, target = in_column(k)
            send(whole.at[own_part], whole.at[own_part], sem, target)

    def owners_done(whole, sem):
        @pl.when(is_owner)
        def _():
            joined(whole, sem, 1).wait_recv()

        @pl.when(jnp.logical_not(is_owner))
        def _():
            joined(whole, sem, 2).wait_recv()

    def owners_left(parts, arrived, whole, first_sem, second_sem):
        @pl.when(is_owner)
        def _():
            joined(parts, first_sem, 1).wait_send()
            joined(arrived, second_sem, rows_z - 1).wait_send()

        @pl.when(jnp.logical_not(is_owner))
        def _():
            joined(parts, first_sem, 2).wait_send()

    barrier = pltpu.get_barrier_semaphore()

    def greet(target):
        pl.semaphore_signal(
            barrier, inc=1, device_id=target, device_id_type=pl.DeviceIdType.MESH
        )

    for k in range(1, COLUMNS):
        greet(in_row(k)[1])
    for k in range(1, rows_z):
        greet(in_column(k)[1])
    for k in range(1, members):
        if k != ranks:
            greet(member(k)[1])
    greet({"grp": (1 - z_hi) * 2 + core})

    loads[0].wait()
    loads[1].wait()
    wide = placed.shape[0]
    begin = seq * depth
    offset = begin % 128
    placed[...] = jnp.zeros(placed.shape, BF16)
    placed[pl.ds(pl.multiple_of(offset, 32), depth), :] = output_ref[...]
    folded = jnp.dot(
        velocity_ref[:, pl.ds(pl.multiple_of(begin - offset, 128), wide)],
        placed[...],
        preferred_element_type=F32,
    )
    fold_out[0] = folded[:, :HEAD_WIDTH]
    fold_out[1] = folded[:, HEAD_WIDTH:]
    fold_column[y] = fold_out[side]

    pl.semaphore_wait(barrier, 1 + COLUMNS - 1 + rows_z - 1 + members - 2)

    send(key_hbm.at[:, other_columns], k_weights.at[mine, z], 0, here)
    for k in range(1, COLUMNS):
        other, target = in_row(k)
        send(fold_out.at[other // 2], fold_column.at[y], 2, target)
    send(query_hbm.at[:, other_columns], q_weights.at[mine, z], 13, here)
    send(value_hbm.at[:, other_columns], value_mail, 1, here)
    send(down_hbm, down_mail, 14, here)
    loads[2].wait()
    loads[3].wait()

    chunk = 16

    def student_rows(i, carry):
        rows = pl.ds(pl.multiple_of(i * chunk, chunk), chunk)
        value = student_ref[rows, :].astype(F32)
        scale = lax.rsqrt(jnp.mean(value * value, axis=-1, keepdims=True) + EPS)
        act_student[rows, :] = (value * scale * student_gain_ref[...]).astype(BF16)
        return carry

    lax.fori_loop(0, tokens // chunk, student_rows, 0)

    def came(src, dst, sem):
        copy_to(src, dst, one_send.at[sem], one_recv.at[sem], here).wait_recv()

    def two_slots(ref):
        return lambda p, r: ref.at[pl.ds(2 * p, 2), r]

    kw = Chain(two_slots(k_weights), kw_send, kw_recv, rows_z)
    qw = Chain(two_slots(q_weights), qw_send, qw_recv, rows_z)
    vw = Chain(lambda p, r: v_weights.at[p, r], vw_send, vw_recv, rows_z)
    dw = Chain(lambda p, r: down_weights.at[p], dw_send, dw_recv, rows_z, rank)
    loads[4].wait()
    came(key_hbm.at[:, other_columns], k_weights.at[theirs, z], 0)
    kw.own()

    joined(fold_column, 2, COLUMNS - 1).wait_recv()
    fold_rows[...] = jnp.sum(fold_column[...], axis=0).reshape(fold_rows.shape)
    to_owners(fold_rows, fold_arrived, 3)
    loads[5].wait()
    came(query_hbm.at[:, other_columns], q_weights.at[theirs, z], 13)
    qw.own()

    def in_order(own, other):
        lower = jnp.where(side == 0, own, other)
        upper = jnp.where(side == 0, other, own)
        return jnp.concatenate([lower, upper], axis=1).astype(BF16)

    loads[12].wait()
    came(down_hbm, down_mail, 14)

    @pl.when(z == rank)
    def _():
        down_weights[pair] = in_order(
            down_own[...].astype(F32).T, down_mail[...].astype(F32).T
        )

    dw.own()
    loads[6].wait()
    loads[7].wait()

    level = noise_level_of(timestep_ref)
    latent = lax.dot_general(
        act_student[...],
        student_head_ref[...],
        (((1,), (1,)), ((), ())),
        preferred_element_type=F32,
    )
    noise = noise_ref[...].astype(F32).T
    noisy = ((1.0 - level) * latent + level * noise).astype(BF16)
    loads[8].wait()
    loads[9].wait()
    slab = 512 if width % 512 == 0 else width

    def hidden_columns(i, carry):
        part = pl.ds(pl.multiple_of(i * slab, slab), slab)
        hidden[:, part] = jnp.dot(
            noisy, patch_ref[:, part], preferred_element_type=F32
        ) + context_ref[:, part].astype(F32)
        return carry

    lax.fori_loop(0, width // slab, hidden_columns, 0)

    kw.step(1)
    @pl.when(is_owner)
    def _():
        fold_whole[own_part] = own_sum(fold_rows, fold_arrived, 3)
        from_owner(fold_whole, 4)

    loads[10].wait()

    def act_rows(i, carry):
        rows = pl.ds(pl.multiple_of(i * chunk, chunk), chunk)
        value = hidden[rows, :]
        scale = lax.rsqrt(jnp.mean(value * value, axis=-1, keepdims=True) + EPS)
        act[side, rows, :] = (value * scale * gain_ref[...]).astype(BF16)
        return carry

    lax.fori_loop(0, tokens // chunk, act_rows, 0)
    half = tokens // 2
    this_half = pl.ds(pl.multiple_of(core * half, half), half)
    that_half = pl.ds(pl.multiple_of((1 - core) * half, half), half)
    send(act.at[side, this_half], act.at[side, this_half], 5, here)
    qw.step(1)
    kw.step(2)

    owners_done(fold_whole, 4)
    whole = fold_whole[...].reshape(LAT, HEAD_WIDTH)
    high = whole.astype(BF16)
    rest = (whole - high.astype(F32)).astype(BF16)
    split = jnp.concatenate([high, rest], axis=0)
    loads[11].wait()
    came(value_hbm.at[:, other_columns], value_mail, 1)

    def fold_value(ref):
        moved = lax.dot_general(
            ref[...], split, (((1,), (1,)), ((), ())), preferred_element_type=F32
        )
        return moved[:, :LAT] + moved[:, LAT:]

    v_weights[pair, z] = in_order(fold_value(value_own), fold_value(value_mail))
    vw.own()
    qw.step(2)

    taken = pl.ds(pl.multiple_of(rank * 16, 16), 16)
    latents[0] = latent
    latents[1] = noisy.astype(F32)
    parts = jnp.concatenate(three_parts(hidden[taken, :]), axis=0)
    residual = lax.dot_general(
        parts, velocity_ref[...], (((1,), (1,)), ((), ())), preferred_element_type=F32
    )
    residual = residual[0:16] + residual[16:32] + residual[32:48]

    def weight_steps(t, carry):
        kw.step(t + 2)
        vw.step(t)
        qw.step(t + 2)
        dw.step(t)
        return carry

    middle = min(4, rows_z)
    lax.fori_loop(1, middle, weight_steps, 0)
    came(act.at[1 - side, this_half], act.at[1 - side, this_half], 5)
    core_mate = {"grp": grp + 1 - 2 * core}
    send(act.at[1 - side, this_half], act.at[1 - side, this_half], 15, core_mate)
    lax.fori_loop(middle, rows_z, weight_steps, 0)
    came(act.at[1 - side, that_half], act.at[1 - side, that_half], 15)

    def rows_at(column):
        part = pl.ds(pl.multiple_of(column * span, span), span)
        return act[:, :, part].reshape(2 * tokens, span)

    def project(weights, p):
        lower = jnp.dot(
            rows_at(p), weights[2 * p].reshape(span, 128), preferred_element_type=F32
        )
        upper = jnp.dot(
            rows_at(3 - p), weights[2 * p + 1].reshape(span, 128), preferred_element_type=F32
        )
        return lower + upper

    def project_packed(weights, p):
        packed = weights[p].reshape(span, 128)
        lower = jnp.dot(rows_at(p), packed, preferred_element_type=F32)
        upper = jnp.dot(rows_at(3 - p), packed, preferred_element_type=F32)
        return lower[:, :LAT] + upper[:, LAT:]

    k_product[...] = project(k_weights, pair)
    kw.sibling_recv()
    keys[pair, z] = (k_product[...] + project(k_weights, 1 - pair)).astype(BF16)
    ka = Chain(lambda p, r: keys.at[p, r, pl.ds(0, tokens)], ka_send, ka_recv, rows_z)
    kb = Chain(lambda p, r: keys.at[p, r, pl.ds(tokens, tokens)], kb_send, kb_recv, rows_z)
    vs = Chain(lambda p, r: values.at[p, r], v_send, v_recv, rows_z)
    ka.own()
    kb.own()
    dw.sibling_recv()
    row = jnp.minimum(rank, rows_z - 1)
    shift = (row * depth) % 128
    down_placed[...] = jnp.zeros(down_placed.shape, BF16)
    for p in range(2):
        down_placed[p, pl.ds(pl.multiple_of(shift, 32), depth), :] = down_weights[p]

    def low_term(column, p):
        part = pl.ds(pl.multiple_of(column * span + row * depth - shift, 128), wide)
        rows = act[:, :, part].reshape(2 * tokens, wide)
        return jnp.dot(rows, down_placed[p], preferred_element_type=F32)

    low_sum = (
        low_term(0, 0)[:, :LAT]
        + low_term(3, 0)[:, LAT:]
        + low_term(1, 1)[:, :LAT]
        + low_term(2, 1)[:, LAT:]
    )
    low_sum = jnp.where(rank < rows_z, low_sum, 0.0)
    low_out[...] = jnp.concatenate([low_sum[:tokens], low_sum[tokens:]], axis=1).reshape(
        low_out.shape
    )
    for k in range(1, ranks):
        send(low_out.at[(rank + k) % ranks], low_in.at[rank], 16, fellow(k))
    low_in[rank] = low_out[rank]
    v_product[...] = project_packed(v_weights, pair)
    vw.sibling_recv()
    moved = (v_product[...] + project_packed(v_weights, 1 - pair)).astype(BF16)
    values[pair, z] = jnp.concatenate([moved[:tokens], moved[tokens:]], axis=1)
    vs.own()
    joined(low_in, 16, ranks - 1).wait_recv()
    low_tiles[rank] = jnp.sum(low_in[...], axis=0).astype(BF16)
    for k in range(1, ranks):
        send(low_tiles.at[rank], low_tiles.at[rank], 17, fellow(k))
    q_product[...] = project(q_weights, pair)
    qw.sibling_recv()
    plain = q_product[...] + project(q_weights, 1 - pair)
    ka.step(1)
    kb.step(1)
    vs.step(1)
    joined(low_tiles, 17, ranks - 1).wait_recv()
    low = low_tiles[...].reshape(tokens, 2 * LAT)
    low = jnp.concatenate([low[:, :LAT], low[:, LAT:]], axis=0)
    loads[13].wait()
    fake = plain + jnp.dot(low, up_ref[:, own_columns], preferred_element_type=F32)
    asked = jnp.concatenate([plain, fake], axis=0).astype(BF16)
    top[...] = jnp.full(top.shape, -1e30, F32)
    factor = HEAD_WIDTH**-0.5

    def score_unit(p, r):
        found = (
            lax.dot_general(
                asked, keys[p, r], (((1,), (1,)), ((), ())), preferred_element_type=F32
            )
            * factor
        )
        scores[p * rows_z + r] = found
        top[...] = jnp.maximum(
            top[...], jnp.maximum(found[:, :tokens], found[:, tokens:])
        )

    def kv_steps(t, carry):
        ka.step(t + 1)
        kb.step(t + 1)
        vs.step(t + 1)

        def way(d, carry):
            r = z + (1 - 2 * d) * (t - 1)
            fits = jnp.logical_and(r >= 0, r < rows_z)

            @pl.when(jnp.logical_and(fits, jnp.logical_or(t > 1, d == 0)))
            def _():
                score_unit(pair, r)

            return carry

        lax.fori_loop(0, 2, way, 0)
        return carry

    lax.fori_loop(1, rows_z + 1, kv_steps, 0)

    def from_sibling(r, carry):
        ka.copy(1 - pair, r, 2, sibling).wait_recv()
        kb.copy(1 - pair, r, 2, sibling).wait_recv()
        score_unit(1 - pair, r)
        return carry

    lax.fori_loop(0, rows_z, from_sibling, 0)
    vs.sibling_recv()
    peak = jnp.max(top[...], axis=-1, keepdims=True)
    top[...] = jnp.broadcast_to(peak, top.shape)
    total[...] = jnp.zeros(total.shape, F32)
    mixed[...] = jnp.zeros(mixed.shape, F32)

    def mix_unit(u, carry):
        shift = top[...]
        left = jnp.exp(scores[u, :, 0:tokens] - shift)
        right = jnp.exp(scores[u, :, tokens : 2 * tokens] - shift)
        total[...] += left + right
        packed = values[u // rows_z, u % rows_z]
        stacked = jnp.concatenate([packed[:, :LAT], packed[:, LAT:]], axis=0)
        mixed[...] += jnp.dot(
            jnp.concatenate([left, right], axis=1).astype(BF16),
            stacked,
            preferred_element_type=F32,
        )
        return carry

    lax.fori_loop(0, 2 * rows_z, mix_unit, 0)
    attended = mixed[...] / jnp.sum(total[...], axis=-1, keepdims=True)
    share[...] = jnp.concatenate(
        [attended[: 2 * tokens], attended[2 * tokens :]], axis=1
    ).reshape(share.shape)

    for k in range(1, members):
        j, target = member(k)
        send(share.at[j], met.at[me], 6, target)
    met[me] = share[me]
    kw.drain()
    dw.drain()
    joined(met, 6, members - 1).wait_recv()
    halves[0] = jnp.sum(met[...], axis=0)
    send(halves.at[0], halves.at[1], 7, {"grp": (1 - z_hi) * 2 + core})
    qw.drain()
    vw.drain()
    ka.drain()
    joined(halves, 7, 1).wait_recv()
    shares = halves[0] + halves[1]
    taken_latent = latents[0, taken, :]
    taken_noisy = latents[1, taken, :]
    real = taken_noisy - level * (residual + shares[:, :LAT])
    fake_pred = taken_noisy - level * (residual + shares[:, LAT:])
    tiles[rank] = jnp.concatenate(
        [fake_pred - real, jnp.abs(taken_latent - real)], axis=1
    )
    for k in range(1, ranks):
        send(tiles.at[rank], tiles.at[rank], 8, fellow(k))
    kb.drain()
    joined(tiles, 8, ranks - 1).wait_recv()
    all_tiles = tiles[...]
    gap = jnp.sum(all_tiles, axis=0)
    gap = gap[0:8] + gap[8:16]
    lane = lax.broadcasted_iota(jnp.int32, gap.shape, 1)
    gap = jnp.where(lane >= LAT, gap, 0.0)
    diff = all_tiles.reshape(tokens, 128)[:, :LAT]

    grad_rows = grad_ref.shape[0]
    start, skip = group * grad_rows, 0
    if grad_rows % 128:
        skip = (group % 2) * LAT
        start = start - skip
    found = lax.dot_general(
        act_student[:, pl.ds(pl.multiple_of(start, 128), window.shape[0])],
        jnp.concatenate(three_parts(diff), axis=1),
        (((0,), (0,)), ((), ())),
        preferred_element_type=F32,
    )
    window[...] = found[:, :LAT] + found[:, LAT : 2 * LAT] + found[:, 2 * LAT :]
    quarter = grad_rows // 8
    for column in range(COLUMNS):
        low_rows = pl.multiple_of(skip + column * quarter, 8)
        high_rows = pl.multiple_of(skip + grad_rows // 2 + column * quarter, 8)
        y_out[column, 0:quarter, :] = jnp.concatenate(
            [window[pl.ds(low_rows, quarter), :], window[pl.ds(high_rows, quarter), :]],
            axis=1,
        )
        y_out[column, quarter : quarter + 8, :] = gap
    for k in range(1, COLUMNS):
        other, target = in_row(k)
        send(y_out.at[other], y_in.at[y], 9, target)
    def left(src, dst, sem):
        copy_to(src, dst, one_send.at[sem], one_recv.at[sem], here).wait_send()

    left(key_hbm.at[:, other_columns], k_weights.at[mine, z], 0)
    left(query_hbm.at[:, other_columns], q_weights.at[mine, z], 13)
    left(value_hbm.at[:, other_columns], value_mail, 1)
    left(down_hbm, down_mail, 14)
    joined(low_out, 16, ranks - 1).wait_send()
    joined(low_tiles, 17, ranks - 1).wait_send()
    left(act.at[side, this_half], act.at[side, this_half], 5)
    left(act.at[1 - side, this_half], act.at[1 - side, this_half], 15)
    y_in[y] = y_out[y]
    joined(y_in, 9, COLUMNS - 1).wait_recv()
    sums = jnp.sum(y_in[...], axis=0)
    share_rows = z_out.shape[1] - 8
    z_out[0, 0:share_rows, :] = sums[0:share_rows]
    z_out[1, 0 : quarter - share_rows, :] = sums[share_rows:quarter]
    if quarter < 2 * share_rows:
        z_out[1, quarter - share_rows : share_rows, :] = jnp.zeros(
            (2 * share_rows - quarter, 128), F32
        )
    for o in range(2):
        z_out[o, share_rows : share_rows + 8, :] = sums[quarter:]
    to_owners(z_out, z_in, 10)
    token_scale = float(tokens * seqs) ** -0.5
    vs.drain()
    joined(fold_column, 2, COLUMNS - 1).wait_send()
    owners_left(fold_rows, fold_arrived, fold_whole, 3, 4)

    @pl.when(is_owner)
    def _():
        summed = own_sum(z_out, z_in, 10)
        gap_total = jnp.sum(summed[share_rows:], keepdims=True)
        factor = 1.0 / (gap_total / (tokens * seqs * LAT) + 1e-05)
        pieces[own_part, 0:share_rows, :] = (factor * token_scale) * summed[0:share_rows]
        pieces[own_part, share_rows : share_rows + 8, :] = jnp.broadcast_to(factor, (8, 128))
        from_owner(pieces, 11)

    owners_done(pieces, 11)
    scale = pieces[0, share_rows : share_rows + 1, 0:1]
    columns[y, 0:share_rows, :] = pieces[0, 0:share_rows, :]
    columns[y, share_rows:quarter, :] = pieces[1, 0 : quarter - share_rows, :]
    for k in range(1, COLUMNS):
        _, target = in_row(k)
        send(columns.at[y], columns.at[y], 12, target)
    diff_ref[...] = scale * diff
    joined(columns, 12, COLUMNS - 1).wait_recv()
    complete = columns[...].reshape(grad_rows // 2, 128)
    grad_ref[0 : grad_rows // 2, :] = complete[:, :LAT]
    grad_ref[grad_rows // 2 :, :] = complete[:, LAT:]

    joined(share, 6, members - 1).wait_send()
    joined(halves, 7, 1).wait_send()
    joined(tiles, 8, ranks - 1).wait_send()
    joined(y_out, 9, COLUMNS - 1).wait_send()
    owners_left(z_out, z_in, pieces, 10, 11)
    joined(columns, 12, COLUMNS - 1).wait_send()


def local(
    student_hidden_states,
    student_norm_gain,
    student_output_head,
    noise,
    timestep,
    context,
    patch_embedding_input,
    attention_norm_gain,
    query_weight,
    key_weight,
    value_weight,
    adapter_down_weight,
    adapter_up_weight,
    output_weight,
    velocity_head_output,
):
    tokens, width = student_hidden_states.shape
    depth = query_weight.shape[0]
    seqs = lax.axis_size("seq")
    rows_z = seqs // COLUMNS
    groups = lax.axis_size("grp") * lax.axis_size("tp")
    ranks = 2 * lax.axis_size("tp")
    grad_rows = width // groups
    window = grad_rows + LAT if grad_rows % 128 else grad_rows
    quarter = grad_rows // 8
    share_rows = (quarter // 8 + 1) // 2 * 8
    wide = 256 if depth % 128 else depth
    vmem = pl.BlockSpec(memory_space=pltpu.VMEM)
    smem = pl.BlockSpec(memory_space=pltpu.SMEM)
    dma = pltpu.SemaphoreType.DMA
    chain = [dma((3 * rows_z,)), dma((2 * rows_z,))]
    return pl.pallas_call(
        functools.partial(kernel, rows_z),
        out_shape=(
            jax.ShapeDtypeStruct((tokens, LAT), F32),
            jax.ShapeDtypeStruct((grad_rows, LAT), F32),
        ),
        in_specs=[smem] + [pl.BlockSpec(memory_space=pl.ANY)] * 14,
        out_specs=(vmem, vmem),
        scratch_shapes=[
            pltpu.VMEM((tokens, width), BF16),
            pltpu.VMEM((1, width), F32),
            pltpu.VMEM((LAT, width), BF16),
            pltpu.VMEM((LAT, tokens), BF16),
            pltpu.VMEM((tokens, width), BF16),
            pltpu.VMEM((LAT, width), BF16),
            pltpu.VMEM((1, width), F32),
            pltpu.VMEM(adapter_up_weight.shape, BF16),
            pltpu.VMEM((depth, 2 * HEAD_WIDTH), BF16),
            pltpu.VMEM((LAT, width), BF16),
            pltpu.VMEM((LAT, depth), BF16),
            pltpu.VMEM((LAT, depth), BF16),
            pltpu.VMEM((depth, HEAD_WIDTH), BF16),
            pltpu.VMEM((depth, HEAD_WIDTH), BF16),
            pltpu.VMEM((COLUMNS, rows_z, depth, HEAD_WIDTH), BF16),
            pltpu.VMEM((COLUMNS, rows_z, depth, HEAD_WIDTH), BF16),
            pltpu.VMEM((2, rows_z, depth, 2 * LAT), BF16),
            pltpu.VMEM((2, depth, 2 * LAT), BF16),
            pltpu.VMEM((2, wide, 2 * LAT), BF16),
            pltpu.VMEM((wide, 256), BF16),
            pltpu.VMEM((2, LAT, HEAD_WIDTH), F32),
            pltpu.VMEM((COLUMNS, LAT, HEAD_WIDTH), F32),
            pltpu.VMEM((2, LAT // 2, HEAD_WIDTH), F32),
            pltpu.VMEM((rows_z, LAT // 2, HEAD_WIDTH), F32),
            pltpu.VMEM((2, LAT // 2, HEAD_WIDTH), F32),
            pltpu.VMEM((tokens, width), BF16),
            pltpu.VMEM((tokens, width), F32),
            pltpu.VMEM((2, tokens, width), BF16),
            pltpu.VMEM((2, tokens, LAT), F32),
            pltpu.VMEM((2 * tokens, HEAD_WIDTH), F32),
            pltpu.VMEM((2 * tokens, HEAD_WIDTH), F32),
            pltpu.VMEM((2 * tokens, LAT), F32),
            pltpu.VMEM((ranks, tokens // ranks, 2 * LAT), F32),
            pltpu.VMEM((ranks, tokens // ranks, 2 * LAT), F32),
            pltpu.VMEM((ranks, tokens // ranks, 2 * LAT), BF16),
            pltpu.VMEM((2, rows_z, 2 * tokens, HEAD_WIDTH), BF16),
            pltpu.VMEM((2, rows_z, tokens, 128), BF16),
            pltpu.VMEM((2 * rows_z, 4 * tokens, 2 * tokens), F32),
            pltpu.VMEM((4 * tokens, tokens), F32),
            pltpu.VMEM((4 * tokens, tokens), F32),
            pltpu.VMEM((4 * tokens, LAT), F32),
            pltpu.VMEM((2 * ranks, 16, 128), F32),
            pltpu.VMEM((2 * ranks, 16, 128), F32),
            pltpu.VMEM((2, 16, 128), F32),
            pltpu.VMEM((ranks, 16, 128), F32),
            pltpu.VMEM((window, LAT), F32),
            pltpu.VMEM((COLUMNS, quarter + 8, 128), F32),
            pltpu.VMEM((COLUMNS, quarter + 8, 128), F32),
            pltpu.VMEM((2, share_rows + 8, 128), F32),
            pltpu.VMEM((rows_z, share_rows + 8, 128), F32),
            pltpu.VMEM((2, share_rows + 8, 128), F32),
            pltpu.VMEM((COLUMNS, quarter, 128), F32),
        ]
        + chain * 7
        + [dma((18,)), dma((18,)), dma((14,))],
        compiler_params=pltpu.CompilerParams(
            collective_id=0, has_side_effects=True, vmem_limit_bytes=60 * MIB
        ),
    )(
        timestep,
        student_hidden_states,
        student_norm_gain.reshape(1, width),
        student_output_head.T,
        noise.T,
        context,
        patch_embedding_input,
        attention_norm_gain.reshape(1, width),
        query_weight,
        key_weight,
        value_weight,
        adapter_down_weight.T,
        adapter_up_weight,
        output_weight.T,
        velocity_head_output.T,
    )


def solution(mesh):
    heads = P("seq", ("grp", "tp"))
    in_specs = (
        P("seq", None),
        P(),
        P(),
        P("seq", None),
        P(),
        P("seq", None),
        P(),
        P(),
        heads,
        heads,
        heads,
        P("seq", None),
        P(None, ("grp", "tp")),
        P(("grp", "tp"), "seq"),
        P(),
    )
    out_specs = (P("seq", None), P(("grp", "tp"), None))
    return jax.shard_map(local, mesh=mesh, in_specs=in_specs, out_specs=out_specs, check_vma=False)
```

```python
import functools

import jax
import jax.numpy as jnp
from jax import lax
from jax.experimental import pallas as pl
from jax.experimental.pallas import tpu as pltpu
from jax.sharding import PartitionSpec as P

HEAD_WIDTH = 128
LAT = 64
COLUMNS = 4
EPS = 1e-06
F32 = jnp.float32
BF16 = jnp.bfloat16
MIB = 1024 * 1024


def position(rows_z):
    seq = lax.axis_index("seq")
    y, z = seq // rows_z, seq % rows_z
    side = y // 2
    pair = jnp.where(y < 2, y, 3 - y)
    partner = (3 - y) * rows_z + z
    sibling = (y + 1 - 2 * (y % 2)) * rows_z + z
    return seq, y, z, side, pair, partner, sibling


def copy_to(src, dst, send_sem, recv_sem, target):
    return pltpu.make_async_remote_copy(
        src_ref=src,
        dst_ref=dst,
        send_sem=send_sem,
        recv_sem=recv_sem,
        device_id=target,
        device_id_type=pl.DeviceIdType.MESH,
    )


class Chain:
    def __init__(self, unit, send_sem, recv_sem, rows_z, only=None):
        self.unit, self.send_sem, self.recv_sem, self.rows_z = unit, send_sem, recv_sem, rows_z
        self.only = only
        (self.seq, _, self.z, _, self.pair, _, self.sibling) = position(rows_z)

    def moves(self, row, condition):
        return condition if self.only is None else jnp.logical_and(condition, row == self.only)

    def copy(self, pair, row, way, target):
        ref = self.unit(pair, row)
        return copy_to(
            ref,
            ref,
            self.send_sem.at[way * self.rows_z + row],
            self.recv_sem.at[pair * self.rows_z + row],
            {"seq": target},
        )

    def up(self, row):
        return self.copy(self.pair, row, 0, jnp.minimum(self.seq + 1, 4 * self.rows_z - 1))

    def down(self, row):
        return self.copy(self.pair, row, 1, jnp.maximum(self.seq - 1, 0))

    def across(self, row):
        return self.copy(self.pair, row, 2, self.sibling)

    def own(self):
        z = self.z

        @pl.when(self.moves(z, z < self.rows_z - 1))
        def _():
            self.up(z).start()

        @pl.when(self.moves(z, z > 0))
        def _():
            self.down(z).start()

        if self.only is None:
            self.across(z).start()
        else:

            @pl.when(z == self.only)
            def _():
                self.across(z).start()

    def step(self, t):
        z, last = self.z, self.rows_z - 1

        @pl.when(self.moves(z - t, z - t >= 0))
        def _():
            row = z - t
            self.up(row).wait_recv()

            @pl.when(z < last)
            def _():
                self.up(row).start()

            self.across(row).start()

        @pl.when(self.moves(z + t, z + t <= last))
        def _():
            row = z + t
            self.down(row).wait_recv()

            @pl.when(z > 0)
            def _():
                self.down(row).start()

            self.across(row).start()

    def sibling_recv(self):
        def body(row, carry):
            @pl.when(self.moves(row, row >= 0))
            def _():
                self.copy(1 - self.pair, row, 2, self.sibling).wait_recv()

            return carry

        lax.fori_loop(0, self.rows_z, body, 0)

    def drain(self):
        z, last = self.z, self.rows_z - 1

        def body(row, carry):
            @pl.when(self.moves(row, jnp.logical_and(z < last, row <= z)))
            def _():
                self.up(row).wait_send()

            @pl.when(self.moves(row, jnp.logical_and(z > 0, row >= z)))
            def _():
                self.down(row).wait_send()

            @pl.when(self.moves(row, row >= 0))
            def _():
                self.across(row).wait_send()

            return carry

        lax.fori_loop(0, self.rows_z, body, 0)


def noise_level_of(timestep_ref):
    fraction = jnp.full((1, LAT), timestep_ref[0], jnp.int32).astype(F32) / 1000.0
    return 5.0 * fraction / (1.0 + 4.0 * fraction)


def three_parts(value):
    high = value.astype(BF16)
    rest = value - high.astype(F32)
    middle = rest.astype(BF16)
    low = (rest - middle.astype(F32)).astype(BF16)
    return high, middle, low


def kernel(
    rows_z,
    timestep_ref,
    student_hbm,
    student_gain_hbm,
    student_head_hbm,
    noise_hbm,
    context_hbm,
    patch_hbm,
    gain_hbm,
    query_hbm,
    key_hbm,
    value_hbm,
    down_hbm,
    up_hbm,
    output_hbm,
    velocity_hbm,
    diff_ref,
    grad_ref,
    student_ref,
    student_gain_ref,
    student_head_ref,
    noise_ref,
    context_ref,
    patch_ref,
    gain_ref,
    up_ref,
    output_ref,
    velocity_ref,
    down_own,
    down_mail,
    value_own,
    value_mail,
    k_weights,
    q_weights,
    v_weights,
    down_weights,
    down_placed,
    placed,
    fold_out,
    fold_column,
    fold_rows,
    fold_arrived,
    fold_whole,
    act_student,
    hidden,
    act,
    latents,
    k_product,
    q_product,
    v_product,
    low_out,
    low_in,
    low_tiles,
    keys,
    values,
    scores,
    top,
    total,
    mixed,
    share,
    met,
    halves,
    tiles,
    window,
    y_out,
    y_in,
    z_out,
    z_in,
    pieces,
    columns,
    kw_send,
    kw_recv,
    qw_send,
    qw_recv,
    vw_send,
    vw_recv,
    dw_send,
    dw_recv,
    ka_send,
    ka_recv,
    kb_send,
    kb_recv,
    v_send,
    v_recv,
    one_send,
    one_recv,
    load_sem,
):
    seq, y, z, side, pair, partner, sibling = position(rows_z)
    tokens, width = student_ref.shape
    depth = query_hbm.shape[0]
    tp_size = lax.axis_size("tp")
    tp = lax.axis_index("tp")
    grp = lax.axis_index("grp")
    groups = lax.axis_size("grp") * tp_size
    group = grp * tp_size + tp
    z_hi, core = grp // 2, grp % 2
    ranks = 2 * tp_size
    rank = core * tp_size + tp
    members = 2 * ranks
    me = side * ranks + rank
    span = width // COLUMNS
    seqs = COLUMNS * rows_z
    here = {"seq": partner}

    def member(k):
        j = (me + k) % members
        column = jnp.where(j // ranks == 0, pair, 3 - pair)
        r = j % ranks
        return j, {
            "grp": z_hi * 2 + r // tp_size,
            "seq": column * rows_z + z,
            "tp": r % tp_size,
        }

    def fellow(k):
        r = (rank + k) % ranks
        return {"grp": z_hi * 2 + r // tp_size, "tp": r % tp_size}

    def in_column(k):
        other = (z + k) % rows_z
        return other, {"seq": y * rows_z + other}

    def in_row(k):
        other = (y + k) % COLUMNS
        return other, {"seq": other * rows_z + z}

    def joined(ref, sem, count):
        part = ref.at[pl.ds(0, count)]
        return copy_to(part, part, one_send.at[sem], one_recv.at[sem], here)

    def send(src, dst, sem, target):
        copy_to(src, dst, one_send.at[sem], one_recv.at[sem], target).start()

    own_columns = pl.ds(pl.multiple_of(side * HEAD_WIDTH, HEAD_WIDTH), HEAD_WIDTH)
    other_columns = pl.ds(pl.multiple_of((1 - side) * HEAD_WIDTH, HEAD_WIDTH), HEAD_WIDTH)
    mine = 2 * pair + side
    theirs = 2 * pair + 1 - side
    sources = (
        (output_hbm, output_ref),
        (velocity_hbm, velocity_ref),
        (student_hbm, student_ref),
        (student_gain_hbm, student_gain_ref),
        (key_hbm.at[:, own_columns], k_weights.at[mine, z]),
        (query_hbm.at[:, own_columns], q_weights.at[mine, z]),
        (student_head_hbm, student_head_ref),
        (noise_hbm, noise_ref),
        (patch_hbm, patch_ref),
        (context_hbm, context_ref),
        (gain_hbm, gain_ref),
        (value_hbm.at[:, own_columns], value_own),
        (down_hbm, down_own),
        (up_hbm, up_ref),
    )
    loads = [
        pltpu.make_async_copy(src, dst, load_sem.at[i]) for i, (src, dst) in enumerate(sources)
    ]
    for load in loads:
        load.start()

    centre = rows_z // 2 - 1
    own_part = jnp.clip(z - centre, 0, 1)
    is_owner = jnp.logical_and(z >= centre, z <= centre + 1)

    def to_owners(parts, arrived, sem):
        for o in range(2):

            @pl.when(z != centre + o)
            def _():
                send(parts.at[o], arrived.at[z], sem, {"seq": y * rows_z + centre + o})

    def own_sum(parts, arrived, sem):
        arrived[z] = parts[own_part]
        joined(arrived, sem, rows_z - 1).wait_recv()
        return jnp.sum(arrived[...], axis=0)

    def from_owner(whole, sem):
        for k in range(1, rows_z):
            _, target = in_column(k)
            send(whole.at[own_part], whole.at[own_part], sem, target)

    def owners_done(whole, sem):
        @pl.when(is_owner)
        def _():
            joined(whole, sem, 1).wait_recv()

        @pl.when(jnp.logical_not(is_owner))
        def _():
            joined(whole, sem, 2).wait_recv()

    def owners_left(parts, arrived, whole, first_sem, second_sem):
        @pl.when(is_owner)
        def _():
            joined(parts, first_sem, 1).wait_send()
            joined(arrived, second_sem, rows_z - 1).wait_send()

        @pl.when(jnp.logical_not(is_owner))
        def _():
            joined(parts, first_sem, 2).wait_send()

    barrier = pltpu.get_barrier_semaphore()

    def greet(target):
        pl.semaphore_signal(
            barrier, inc=1, device_id=target, device_id_type=pl.DeviceIdType.MESH
        )

    for k in range(1, COLUMNS):
        greet(in_row(k)[1])
    for k in range(1, rows_z):
        greet(in_column(k)[1])
    for k in range(1, members):
        if k != ranks:
            greet(member(k)[1])
    greet({"grp": (1 - z_hi) * 2 + core})

    loads[0].wait()
    loads[1].wait()
    wide = placed.shape[0]
    begin = seq * depth
    offset = begin % 128
    placed[...] = jnp.zeros(placed.shape, BF16)
    placed[pl.ds(pl.multiple_of(offset, 32), depth), :] = output_ref[...]
    folded = jnp.dot(
        velocity_ref[:, pl.ds(pl.multiple_of(begin - offset, 128), wide)],
        placed[...],
        preferred_element_type=F32,
    )
    fold_out[0] = folded[:, :HEAD_WIDTH]
    fold_out[1] = folded[:, HEAD_WIDTH:]
    fold_column[y] = fold_out[side]

    pl.semaphore_wait(barrier, 1 + COLUMNS - 1 + rows_z - 1 + members - 2)

    send(key_hbm.at[:, other_columns], k_weights.at[mine, z], 0, here)
    for k in range(1, COLUMNS):
        other, target = in_row(k)
        send(fold_out.at[other // 2], fold_column.at[y], 2, target)
    send(query_hbm.at[:, other_columns], q_weights.at[mine, z], 13, here)
    send(value_hbm.at[:, other_columns], value_mail, 1, here)
    send(down_hbm, down_mail, 14, here)
    loads[2].wait()
    loads[3].wait()

    chunk = 16

    def student_rows(i, carry):
        rows = pl.ds(pl.multiple_of(i * chunk, chunk), chunk)
        value = student_ref[rows, :].astype(F32)
        scale = lax.rsqrt(jnp.mean(value * value, axis=-1, keepdims=True) + EPS)
        act_student[rows, :] = (value * scale * student_gain_ref[...]).astype(BF16)
        return carry

    lax.fori_loop(0, tokens // chunk, student_rows, 0)

    def came(src, dst, sem):
        copy_to(src, dst, one_send.at[sem], one_recv.at[sem], here).wait_recv()

    def two_slots(ref):
        return lambda p, r: ref.at[pl.ds(2 * p, 2), r]

    kw = Chain(two_slots(k_weights), kw_send, kw_recv, rows_z)
    qw = Chain(two_slots(q_weights), qw_send, qw_recv, rows_z)
    vw = Chain(lambda p, r: v_weights.at[p, r], vw_send, vw_recv, rows_z)
    dw = Chain(lambda p, r: down_weights.at[p], dw_send, dw_recv, rows_z, rank)
    loads[4].wait()
    came(key_hbm.at[:, other_columns], k_weights.at[theirs, z], 0)
    kw.own()

    joined(fold_column, 2, COLUMNS - 1).wait_recv()
    fold_rows[...] = jnp.sum(fold_column[...], axis=0).reshape(fold_rows.shape)
    to_owners(fold_rows, fold_arrived, 3)
    loads[5].wait()
    came(query_hbm.at[:, other_columns], q_weights.at[theirs, z], 13)
    qw.own()

    def in_order(own, other):
        lower = jnp.where(side == 0, own, other)
        upper = jnp.where(side == 0, other, own)
        return jnp.concatenate([lower, upper], axis=1).astype(BF16)

    loads[12].wait()
    came(down_hbm, down_mail, 14)

    @pl.when(z == rank)
    def _():
        down_weights[pair] = in_order(
            down_own[...].astype(F32).T, down_mail[...].astype(F32).T
        )

    dw.own()
    loads[6].wait()
    loads[7].wait()

    level = noise_level_of(timestep_ref)
    latent = lax.dot_general(
        act_student[...],
        student_head_ref[...],
        (((1,), (1,)), ((), ())),
        preferred_element_type=F32,
    )
    noise = noise_ref[...].astype(F32).T
    noisy = ((1.0 - level) * latent + level * noise).astype(BF16)
    loads[8].wait()
    loads[9].wait()
    slab = 512 if width % 512 == 0 else width

    def hidden_columns(i, carry):
        part = pl.ds(pl.multiple_of(i * slab, slab), slab)
        hidden[:, part] = jnp.dot(
            noisy, patch_ref[:, part], preferred_element_type=F32
        ) + context_ref[:, part].astype(F32)
        return carry

    lax.fori_loop(0, width // slab, hidden_columns, 0)

    kw.step(1)
    @pl.when(is_owner)
    def _():
        fold_whole[own_part] = own_sum(fold_rows, fold_arrived, 3)
        from_owner(fold_whole, 4)

    loads[10].wait()

    def act_rows(i, carry):
        rows = pl.ds(pl.multiple_of(i * chunk, chunk), chunk)
        value = hidden[rows, :]
        scale = lax.rsqrt(jnp.mean(value * value, axis=-1, keepdims=True) + EPS)
        act[side, rows, :] = (value * scale * gain_ref[...]).astype(BF16)
        return carry

    lax.fori_loop(0, tokens // chunk, act_rows, 0)
    half = tokens // 2
    this_half = pl.ds(pl.multiple_of(core * half, half), half)
    that_half = pl.ds(pl.multiple_of((1 - core) * half, half), half)
    send(act.at[side, this_half], act.at[side, this_half], 5, here)
    qw.step(1)
    kw.step(2)

    owners_done(fold_whole, 4)
    whole = fold_whole[...].reshape(LAT, HEAD_WIDTH)
    high = whole.astype(BF16)
    rest = (whole - high.astype(F32)).astype(BF16)
    split = jnp.concatenate([high, rest], axis=0)
    loads[11].wait()
    came(value_hbm.at[:, other_columns], value_mail, 1)

    def fold_value(ref):
        moved = lax.dot_general(
            ref[...], split, (((1,), (1,)), ((), ())), preferred_element_type=F32
        )
        return moved[:, :LAT] + moved[:, LAT:]

    v_weights[pair, z] = in_order(fold_value(value_own), fold_value(value_mail))
    vw.own()
    qw.step(2)

    taken = pl.ds(pl.multiple_of(rank * 16, 16), 16)
    latents[0] = latent
    latents[1] = noisy.astype(F32)
    parts = jnp.concatenate(three_parts(hidden[taken, :]), axis=0)
    residual = lax.dot_general(
        parts, velocity_ref[...], (((1,), (1,)), ((), ())), preferred_element_type=F32
    )
    residual = residual[0:16] + residual[16:32] + residual[32:48]

    def weight_steps(t, carry):
        kw.step(t + 2)
        vw.step(t)
        qw.step(t + 2)
        dw.step(t)
        return carry

    middle = min(4, rows_z)
    lax.fori_loop(1, middle, weight_steps, 0)
    came(act.at[1 - side, this_half], act.at[1 - side, this_half], 5)
    core_mate = {"grp": grp + 1 - 2 * core}
    send(act.at[1 - side, this_half], act.at[1 - side, this_half], 15, core_mate)
    lax.fori_loop(middle, rows_z, weight_steps, 0)
    came(act.at[1 - side, that_half], act.at[1 - side, that_half], 15)

    def rows_at(column):
        part = pl.ds(pl.multiple_of(column * span, span), span)
        return act[:, :, part].reshape(2 * tokens, span)

    def project(weights, p):
        lower = jnp.dot(
            rows_at(p), weights[2 * p].reshape(span, 128), preferred_element_type=F32
        )
        upper = jnp.dot(
            rows_at(3 - p), weights[2 * p + 1].reshape(span, 128), preferred_element_type=F32
        )
        return lower + upper

    def project_packed(weights, p):
        packed = weights[p].reshape(span, 128)
        lower = jnp.dot(rows_at(p), packed, preferred_element_type=F32)
        upper = jnp.dot(rows_at(3 - p), packed, preferred_element_type=F32)
        return lower[:, :LAT] + upper[:, LAT:]

    k_product[...] = project(k_weights, pair)
    kw.sibling_recv()
    keys[pair, z] = (k_product[...] + project(k_weights, 1 - pair)).astype(BF16)
    ka = Chain(lambda p, r: keys.at[p, r, pl.ds(0, tokens)], ka_send, ka_recv, rows_z)
    kb = Chain(lambda p, r: keys.at[p, r, pl.ds(tokens, tokens)], kb_send, kb_recv, rows_z)
    vs = Chain(lambda p, r: values.at[p, r], v_send, v_recv, rows_z)
    ka.own()
    kb.own()
    dw.sibling_recv()
    row = jnp.minimum(rank, rows_z - 1)
    shift = (row * depth) % 128
    down_placed[...] = jnp.zeros(down_placed.shape, BF16)
    for p in range(2):
        down_placed[p, pl.ds(pl.multiple_of(shift, 32), depth), :] = down_weights[p]

    def low_term(column, p):
        part = pl.ds(pl.multiple_of(column * span + row * depth - shift, 128), wide)
        rows = act[:, :, part].reshape(2 * tokens, wide)
        return jnp.dot(rows, down_placed[p], preferred_element_type=F32)

    low_sum = (
        low_term(0, 0)[:, :LAT]
        + low_term(3, 0)[:, LAT:]
        + low_term(1, 1)[:, :LAT]
        + low_term(2, 1)[:, LAT:]
    )
    low_sum = jnp.where(rank < rows_z, low_sum, 0.0)
    low_out[...] = jnp.concatenate([low_sum[:tokens], low_sum[tokens:]], axis=1).reshape(
        low_out.shape
    )
    for k in range(1, ranks):
        send(low_out.at[(rank + k) % ranks], low_in.at[rank], 16, fellow(k))
    low_in[rank] = low_out[rank]
    v_product[...] = project_packed(v_weights, pair)
    vw.sibling_recv()
    moved = (v_product[...] + project_packed(v_weights, 1 - pair)).astype(BF16)
    values[pair, z] = jnp.concatenate([moved[:tokens], moved[tokens:]], axis=1)
    vs.own()
    joined(low_in, 16, ranks - 1).wait_recv()
    low_tiles[rank] = jnp.sum(low_in[...], axis=0).astype(BF16)
    for k in range(1, ranks):
        send(low_tiles.at[rank], low_tiles.at[rank], 17, fellow(k))
    q_product[...] = project(q_weights, pair)
    qw.sibling_recv()
    plain = q_product[...] + project(q_weights, 1 - pair)
    ka.step(1)
    kb.step(1)
    vs.step(1)
    joined(low_tiles, 17, ranks - 1).wait_recv()
    low = low_tiles[...].reshape(tokens, 2 * LAT)
    low = jnp.concatenate([low[:, :LAT], low[:, LAT:]], axis=0)
    loads[13].wait()
    fake = plain + jnp.dot(low, up_ref[:, own_columns], preferred_element_type=F32)
    asked = jnp.concatenate([plain, fake], axis=0).astype(BF16)
    top[...] = jnp.full(top.shape, -1e30, F32)
    factor = HEAD_WIDTH**-0.5

    def score_unit(p, r):
        found = (
            lax.dot_general(
                asked, keys[p, r], (((1,), (1,)), ((), ())), preferred_element_type=F32
            )
            * factor
        )
        scores[p * rows_z + r] = found
        top[...] = jnp.maximum(
            top[...], jnp.maximum(found[:, :tokens], found[:, tokens:])
        )

    def kv_steps(t, carry):
        ka.step(t + 1)
        kb.step(t + 1)
        vs.step(t + 1)

        def way(d, carry):
            r = z + (1 - 2 * d) * (t - 1)
            fits = jnp.logical_and(r >= 0, r < rows_z)

            @pl.when(jnp.logical_and(fits, jnp.logical_or(t > 1, d == 0)))
            def _():
                score_unit(pair, r)

            far = z + (1 - 2 * d) * (t - 2)
            near = jnp.logical_and(t == 2, d == 0)
            held = jnp.logical_and(far >= 0, far < rows_z)

            @pl.when(jnp.logical_and(held, jnp.logical_or(t > 2, near)))
            def _():
                ka.copy(1 - pair, far, 2, sibling).wait_recv()
                kb.copy(1 - pair, far, 2, sibling).wait_recv()
                score_unit(1 - pair, far)

            return carry

        lax.fori_loop(0, 2, way, 0)
        return carry

    lax.fori_loop(1, rows_z + 2, kv_steps, 0)

    vs.sibling_recv()
    peak = jnp.max(top[...], axis=-1, keepdims=True)
    top[...] = jnp.broadcast_to(peak, top.shape)
    total[...] = jnp.zeros(total.shape, F32)
    mixed[...] = jnp.zeros(mixed.shape, F32)

    def mix_unit(u, carry):
        shift = top[...]
        left = jnp.exp(scores[u, :, 0:tokens] - shift)
        right = jnp.exp(scores[u, :, tokens : 2 * tokens] - shift)
        total[...] += left + right
        packed = values[u // rows_z, u % rows_z]
        stacked = jnp.concatenate([packed[:, :LAT], packed[:, LAT:]], axis=0)
        mixed[...] += jnp.dot(
            jnp.concatenate([left, right], axis=1).astype(BF16),
            stacked,
            preferred_element_type=F32,
        )
        return carry

    lax.fori_loop(0, 2 * rows_z, mix_unit, 0)
    attended = mixed[...] / jnp.sum(total[...], axis=-1, keepdims=True)
    share[...] = jnp.concatenate(
        [attended[: 2 * tokens], attended[2 * tokens :]], axis=1
    ).reshape(share.shape)

    for k in range(1, members):
        j, target = member(k)
        send(share.at[j], met.at[me], 6, target)
    met[me] = share[me]
    kw.drain()
    dw.drain()
    joined(met, 6, members - 1).wait_recv()
    halves[0] = jnp.sum(met[...], axis=0)
    send(halves.at[0], halves.at[1], 7, {"grp": (1 - z_hi) * 2 + core})
    qw.drain()
    vw.drain()
    ka.drain()
    joined(halves, 7, 1).wait_recv()
    shares = halves[0] + halves[1]
    taken_latent = latents[0, taken, :]
    taken_noisy = latents[1, taken, :]
    real = taken_noisy - level * (residual + shares[:, :LAT])
    fake_pred = taken_noisy - level * (residual + shares[:, LAT:])
    tiles[rank] = jnp.concatenate(
        [fake_pred - real, jnp.abs(taken_latent - real)], axis=1
    )
    for k in range(1, ranks):
        send(tiles.at[rank], tiles.at[rank], 8, fellow(k))
    kb.drain()
    joined(tiles, 8, ranks - 1).wait_recv()
    all_tiles = tiles[...]
    gap = jnp.sum(all_tiles, axis=0)
    gap = gap[0:8] + gap[8:16]
    lane = lax.broadcasted_iota(jnp.int32, gap.shape, 1)
    gap = jnp.where(lane >= LAT, gap, 0.0)
    diff = all_tiles.reshape(tokens, 128)[:, :LAT]

    grad_rows = grad_ref.shape[0]
    start, skip = group * grad_rows, 0
    if grad_rows % 128:
        skip = (group % 2) * LAT
        start = start - skip
    found = lax.dot_general(
        act_student[:, pl.ds(pl.multiple_of(start, 128), window.shape[0])],
        jnp.concatenate(three_parts(diff), axis=1),
        (((0,), (0,)), ((), ())),
        preferred_element_type=F32,
    )
    window[...] = found[:, :LAT] + found[:, LAT : 2 * LAT] + found[:, 2 * LAT :]
    quarter = grad_rows // 8
    for column in range(COLUMNS):
        low_rows = pl.multiple_of(skip + column * quarter, 8)
        high_rows = pl.multiple_of(skip + grad_rows // 2 + column * quarter, 8)
        y_out[column, 0:quarter, :] = jnp.concatenate(
            [window[pl.ds(low_rows, quarter), :], window[pl.ds(high_rows, quarter), :]],
            axis=1,
        )
        y_out[column, quarter : quarter + 8, :] = gap
    for k in range(1, COLUMNS):
        other, target = in_row(k)
        send(y_out.at[other], y_in.at[y], 9, target)
    def left(src, dst, sem):
        copy_to(src, dst, one_send.at[sem], one_recv.at[sem], here).wait_send()

    left(key_hbm.at[:, other_columns], k_weights.at[mine, z], 0)
    left(query_hbm.at[:, other_columns], q_weights.at[mine, z], 13)
    left(value_hbm.at[:, other_columns], value_mail, 1)
    left(down_hbm, down_mail, 14)
    joined(low_out, 16, ranks - 1).wait_send()
    joined(low_tiles, 17, ranks - 1).wait_send()
    left(act.at[side, this_half], act.at[side, this_half], 5)
    left(act.at[1 - side, this_half], act.at[1 - side, this_half], 15)
    y_in[y] = y_out[y]
    joined(y_in, 9, COLUMNS - 1).wait_recv()
    sums = jnp.sum(y_in[...], axis=0)
    share_rows = z_out.shape[1] - 8
    z_out[0, 0:share_rows, :] = sums[0:share_rows]
    z_out[1, 0 : quarter - share_rows, :] = sums[share_rows:quarter]
    if quarter < 2 * share_rows:
        z_out[1, quarter - share_rows : share_rows, :] = jnp.zeros(
            (2 * share_rows - quarter, 128), F32
        )
    for o in range(2):
        z_out[o, share_rows : share_rows + 8, :] = sums[quarter:]
    to_owners(z_out, z_in, 10)
    token_scale = float(tokens * seqs) ** -0.5
    vs.drain()
    joined(fold_column, 2, COLUMNS - 1).wait_send()
    owners_left(fold_rows, fold_arrived, fold_whole, 3, 4)

    @pl.when(is_owner)
    def _():
        summed = own_sum(z_out, z_in, 10)
        gap_total = jnp.sum(summed[share_rows:], keepdims=True)
        factor = 1.0 / (gap_total / (tokens * seqs * LAT) + 1e-05)
        pieces[own_part, 0:share_rows, :] = (factor * token_scale) * summed[0:share_rows]
        pieces[own_part, share_rows : share_rows + 8, :] = jnp.broadcast_to(factor, (8, 128))
        from_owner(pieces, 11)

    owners_done(pieces, 11)
    scale = pieces[0, share_rows : share_rows + 1, 0:1]
    columns[y, 0:share_rows, :] = pieces[0, 0:share_rows, :]
    columns[y, share_rows:quarter, :] = pieces[1, 0 : quarter - share_rows, :]
    for k in range(1, COLUMNS):
        _, target = in_row(k)
        send(columns.at[y], columns.at[y], 12, target)
    diff_ref[...] = scale * diff
    joined(columns, 12, COLUMNS - 1).wait_recv()
    complete = columns[...].reshape(grad_rows // 2, 128)
    grad_ref[0 : grad_rows // 2, :] = complete[:, :LAT]
    grad_ref[grad_rows // 2 :, :] = complete[:, LAT:]

    joined(share, 6, members - 1).wait_send()
    joined(halves, 7, 1).wait_send()
    joined(tiles, 8, ranks - 1).wait_send()
    joined(y_out, 9, COLUMNS - 1).wait_send()
    owners_left(z_out, z_in, pieces, 10, 11)
    joined(columns, 12, COLUMNS - 1).wait_send()


def local(
    student_hidden_states,
    student_norm_gain,
    student_output_head,
    noise,
    timestep,
    context,
    patch_embedding_input,
    attention_norm_gain,
    query_weight,
    key_weight,
    value_weight,
    adapter_down_weight,
    adapter_up_weight,
    output_weight,
    velocity_head_output,
):
    tokens, width = student_hidden_states.shape
    depth = query_weight.shape[0]
    seqs = lax.axis_size("seq")
    rows_z = seqs // COLUMNS
    groups = lax.axis_size("grp") * lax.axis_size("tp")
    ranks = 2 * lax.axis_size("tp")
    grad_rows = width // groups
    window = grad_rows + LAT if grad_rows % 128 else grad_rows
    quarter = grad_rows // 8
    share_rows = (quarter // 8 + 1) // 2 * 8
    wide = 256 if depth % 128 else depth
    vmem = pl.BlockSpec(memory_space=pltpu.VMEM)
    smem = pl.BlockSpec(memory_space=pltpu.SMEM)
    dma = pltpu.SemaphoreType.DMA
    chain = [dma((3 * rows_z,)), dma((2 * rows_z,))]
    return pl.pallas_call(
        functools.partial(kernel, rows_z),
        out_shape=(
            jax.ShapeDtypeStruct((tokens, LAT), F32),
            jax.ShapeDtypeStruct((grad_rows, LAT), F32),
        ),
        in_specs=[smem] + [pl.BlockSpec(memory_space=pl.ANY)] * 14,
        out_specs=(vmem, vmem),
        scratch_shapes=[
            pltpu.VMEM((tokens, width), BF16),
            pltpu.VMEM((1, width), F32),
            pltpu.VMEM((LAT, width), BF16),
            pltpu.VMEM((LAT, tokens), BF16),
            pltpu.VMEM((tokens, width), BF16),
            pltpu.VMEM((LAT, width), BF16),
            pltpu.VMEM((1, width), F32),
            pltpu.VMEM(adapter_up_weight.shape, BF16),
            pltpu.VMEM((depth, 2 * HEAD_WIDTH), BF16),
            pltpu.VMEM((LAT, width), BF16),
            pltpu.VMEM((LAT, depth), BF16),
            pltpu.VMEM((LAT, depth), BF16),
            pltpu.VMEM((depth, HEAD_WIDTH), BF16),
            pltpu.VMEM((depth, HEAD_WIDTH), BF16),
            pltpu.VMEM((COLUMNS, rows_z, depth, HEAD_WIDTH), BF16),
            pltpu.VMEM((COLUMNS, rows_z, depth, HEAD_WIDTH), BF16),
            pltpu.VMEM((2, rows_z, depth, 2 * LAT), BF16),
            pltpu.VMEM((2, depth, 2 * LAT), BF16),
            pltpu.VMEM((2, wide, 2 * LAT), BF16),
            pltpu.VMEM((wide, 256), BF16),
            pltpu.VMEM((2, LAT, HEAD_WIDTH), F32),
            pltpu.VMEM((COLUMNS, LAT, HEAD_WIDTH), F32),
            pltpu.VMEM((2, LAT // 2, HEAD_WIDTH), F32),
            pltpu.VMEM((rows_z, LAT // 2, HEAD_WIDTH), F32),
            pltpu.VMEM((2, LAT // 2, HEAD_WIDTH), F32),
            pltpu.VMEM((tokens, width), BF16),
            pltpu.VMEM((tokens, width), F32),
            pltpu.VMEM((2, tokens, width), BF16),
            pltpu.VMEM((2, tokens, LAT), F32),
            pltpu.VMEM((2 * tokens, HEAD_WIDTH), F32),
            pltpu.VMEM((2 * tokens, HEAD_WIDTH), F32),
            pltpu.VMEM((2 * tokens, LAT), F32),
            pltpu.VMEM((ranks, tokens // ranks, 2 * LAT), F32),
            pltpu.VMEM((ranks, tokens // ranks, 2 * LAT), F32),
            pltpu.VMEM((ranks, tokens // ranks, 2 * LAT), BF16),
            pltpu.VMEM((2, rows_z, 2 * tokens, HEAD_WIDTH), BF16),
            pltpu.VMEM((2, rows_z, tokens, 128), BF16),
            pltpu.VMEM((2 * rows_z, 4 * tokens, 2 * tokens), F32),
            pltpu.VMEM((4 * tokens, tokens), F32),
            pltpu.VMEM((4 * tokens, tokens), F32),
            pltpu.VMEM((4 * tokens, LAT), F32),
            pltpu.VMEM((2 * ranks, 16, 128), F32),
            pltpu.VMEM((2 * ranks, 16, 128), F32),
            pltpu.VMEM((2, 16, 128), F32),
            pltpu.VMEM((ranks, 16, 128), F32),
            pltpu.VMEM((window, LAT), F32),
            pltpu.VMEM((COLUMNS, quarter + 8, 128), F32),
            pltpu.VMEM((COLUMNS, quarter + 8, 128), F32),
            pltpu.VMEM((2, share_rows + 8, 128), F32),
            pltpu.VMEM((rows_z, share_rows + 8, 128), F32),
            pltpu.VMEM((2, share_rows + 8, 128), F32),
            pltpu.VMEM((COLUMNS, quarter, 128), F32),
        ]
        + chain * 7
        + [dma((18,)), dma((18,)), dma((14,))],
        compiler_params=pltpu.CompilerParams(
            collective_id=0, has_side_effects=True, vmem_limit_bytes=60 * MIB
        ),
    )(
        timestep,
        student_hidden_states,
        student_norm_gain.reshape(1, width),
        student_output_head.T,
        noise.T,
        context,
        patch_embedding_input,
        attention_norm_gain.reshape(1, width),
        query_weight,
        key_weight,
        value_weight,
        adapter_down_weight.T,
        adapter_up_weight,
        output_weight.T,
        velocity_head_output.T,
    )


def solution(mesh):
    heads = P("seq", ("grp", "tp"))
    in_specs = (
        P("seq", None),
        P(),
        P(),
        P("seq", None),
        P(),
        P("seq", None),
        P(),
        P(),
        heads,
        heads,
        heads,
        P("seq", None),
        P(None, ("grp", "tp")),
        P(("grp", "tp"), "seq"),
        P(),
    )
    out_specs = (P("seq", None), P(("grp", "tp"), None))
    return jax.shard_map(local, mesh=mesh, in_specs=in_specs, out_specs=out_specs, check_vma=False)
```
